256 devices in a mesh: image: 4 (over y), swarm: 16 (over z_hi, x), domain: 4 (over z_lo, core).
Axes of the slice: x: 4, y: 4, z: 8 (z_hi: 4, z_lo: 2; z = z_hi * 2 + z_lo), core: 2. Of those that a mesh axis runs over, the one named last changes fastest.
Arguments:
- configuration: float32 [4, 3, 4, 16384], P('image', None, 'domain', 'swarm'), may hold values from -1 to 1
- velocities: float32 [4, 3, 4, 16, 16384], P('image', None, 'domain', None, 'swarm'), may hold values from -6 to 6
- pairs: int32 [4, 128, 2], P('domain'), may hold values from 0 to 191, as said below
- cv_atoms: int32 [128, 16], replicated, may hold values from 0 to 65535
Outputs:
- final_positions: float32 [4, 16, 3, 4, 16384], P('image', 'swarm', None, 'domain')
- new_string: float32 [4, 3, 128], P('image')
The draws below stay inside these ranges and needn't reach their ends.
Inputs may be any that keep to these rules, and one draw needn't show every extreme that they name: pairs[d, t] names 2 different extended tiles, none of them t + 32 itself, each within 32 tiles of it.
All inputs are finite; a program needn't handle non-finite values.
Results may differ from the reference program's by a relative error of at most 0.000064.
Values sent between devices are 32-bit elements; how exact they have to be, the bound alone decides.
No kernel may reach another device: no remote copies, remote signals or barrier semaphores. Data moves between devices by JAX's collectives and lax.ppermute only.
A program may use at most 128 MiB of HBM per device.

```python
import math
import jax
import jax.numpy as jnp
from jax import lax

A_DEV = 16384
NB = 2
HALO = 4096
NCV = 128
GSIZE = 16
IMAGES = 4
MEMBERS = 16
DOMAINS = 4
ATOMS = 65536


def draw_pairs(key, part):
    key = jax.random.fold_in(key, 7)
    halo_tiles = HALO // 128
    tile_count = A_DEV // 128
    choices_row = 2 * halo_tiles
    scores = jax.random.randint(key, (DOMAINS, tile_count, choices_row), 0, 1 << 20) * choices_row
    scores = scores + jnp.arange(choices_row, dtype=jnp.int32)[None, None, :]
    tile_ids = jnp.arange(tile_count, dtype=jnp.int32)[:, None]
    offsets_ids = jnp.arange(choices_row, dtype=jnp.int32)[None, :]
    lowest = (tile_ids == 0) & (offsets_ids == 0)
    highest = (tile_ids == tile_count - 1) & (offsets_ids == choices_row - 1)
    scores = jnp.where((lowest | highest)[None], -1, scores)
    picked = jnp.argsort(scores, axis=-1, stable=True)[..., :NB].astype(jnp.int32)
    offset = jnp.where(picked < halo_tiles, picked - halo_tiles, picked - halo_tiles + 1)
    return (tile_ids[None] + halo_tiles + offset).astype(jnp.int32)


def plant(entries, own_key, least, high):
    longest = entries.shape.index(max(entries.shape))
    spots = []
    for shift in (0, 1):
        where = [jax.random.randint(jax.random.fold_in(own_key, axis), (), 0, length) for axis, length in enumerate(entries.shape)]
        where[longest] = (where[longest] + shift) % entries.shape[longest]
        spots.append(tuple(where))
    return entries.at[spots[0]].set(least).at[spots[1]].set(high)


def steps_of(rng, shape, split, low, top_value):
    loudness = 1.0
    for dim, shards_of in split:
        draws = jax.random.uniform(jax.random.fold_in(jax.random.fold_in(rng, 6), dim), (shards_of,), jnp.float32, low / len(split), top_value / len(split))
        loudness = loudness * jnp.repeat(jnp.exp(draws), shape[dim] // shards_of).reshape((-1,) + (1,) * (len(shape) - 1 - dim))
    return loudness


def scatter_about(own_key, shape, width, limit, cuts=(), kind=jnp.bfloat16):
    array = width * jax.random.normal(own_key, shape, jnp.float32)
    if cuts:
        array = array * steps_of(own_key, shape, cuts, -0.22, 0.18)
    return jnp.clip(array, -limit, limit).astype(kind)


def setup_inputs(seed: int = 0) -> dict:
    streams_of = jax.random.split(jax.random.key(seed), 5)
    configuration = jnp.clip(jax.random.uniform(streams_of[0], (IMAGES, 3, DOMAINS, A_DEV), jnp.float32, -1.0, 1.0) * steps_of(streams_of[0], (IMAGES, 3, DOMAINS, A_DEV), ((0, 4), (2, 4), (3, 16)), -0.4, 0.0), -1.0, 1.0)
    velocities = scatter_about(streams_of[1], (IMAGES, 3, DOMAINS, MEMBERS, A_DEV), 1.0, 6.0, ((0, 4), (2, 4), (4, 16)), jnp.float32)
    pairs = draw_pairs(jax.random.fold_in(streams_of[4], 71), 0)
    cv_atoms = plant(jax.random.randint(streams_of[3], (NCV, GSIZE), 0, ATOMS), jax.random.fold_in(streams_of[3], 1), 0, ATOMS - 1).astype(jnp.int32)
    return {"configuration": configuration, "velocities": velocities, "pairs": pairs, "cv_atoms": cv_atoms}


time_step = 0.25
cutoff_sq = 2.0
strength = 0.1
smoothing = 0.25


def tile_forces(extended, partners, first_tile, tile_count):
    halo_tiles = HALO // 128
    tile_view = extended.reshape(3, extended.shape[1] // 128, 128)
    block_size = math.gcd(16, tile_count)

    def one_block(block_start):
        own_ids = block_start + jnp.arange(block_size, dtype=jnp.int32)
        listed = lax.dynamic_slice_in_dim(partners, block_start, block_size, 0)
        partner_ids = jnp.concatenate([(own_ids + halo_tiles)[:, None], listed], 1)
        own_rows = jnp.take(tile_view, own_ids + halo_tiles, axis=1)
        others = jnp.take(tile_view, partner_ids, axis=1)
        gap_sq = jnp.zeros((block_size, partner_ids.shape[1], 128, 128), jnp.float32)
        for component in range(3):
            gap = own_rows[component][:, None, :, None] - others[component][:, :, None, :]
            gap_sq = gap_sq + gap * gap
        weight = jnp.square(jnp.maximum(1.0 - gap_sq / cutoff_sq, 0.0))
        row_total = jnp.sum(weight, axis=(1, 3))
        pulled = jnp.einsum("bpij,cbpj->cbi", weight, others, precision=lax.Precision.HIGHEST)
        return strength * (own_rows * row_total[None] - pulled)

    starts = first_tile + block_size * jnp.arange(tile_count // block_size, dtype=jnp.int32)
    blocks_out = lax.map(one_block, starts)
    return jnp.moveaxis(blocks_out, 1, 0).reshape(3, tile_count * 128)


def extend_domains(positions):
    zero_rim = jnp.zeros((1, 3, HALO), jnp.float32)
    lower_rim = jnp.concatenate([zero_rim, positions[:-1, :, positions.shape[2] - HALO:]], 0)
    upper_rim = jnp.concatenate([positions[1:, :, :HALO], zero_rim], 0)
    return jnp.concatenate([lower_rim, positions, upper_rim], 2)


def domain_forces(positions, pairs):
    extended = extend_domains(positions)

    def per_domain(domain_pair):
        return tile_forces(domain_pair[0], domain_pair[1], 0, A_DEV // 128)

    return lax.map(per_domain, (extended, pairs))


def run_member(start_pos, start_vel, pairs):
    velocity = start_vel + time_step * domain_forces(start_pos, pairs)
    middle = start_pos + time_step * velocity
    velocity = velocity + time_step * domain_forces(middle, pairs)
    return middle + time_step * velocity


def reference(configuration, velocities, pairs, cv_atoms):
    layout = jnp.transpose(configuration, (0, 2, 1, 3))
    member_vel = jnp.transpose(velocities, (0, 3, 2, 1, 4)).reshape(IMAGES * MEMBERS, DOMAINS, 3, A_DEV)
    repeated = jnp.repeat(layout, MEMBERS, axis=0)

    def per_member(member_pair):
        return run_member(member_pair[0], member_pair[1], pairs)

    finals = lax.map(per_member, (repeated, member_vel))
    finals = finals.reshape(IMAGES, MEMBERS, DOMAINS, 3, A_DEV)
    final_positions = jnp.transpose(finals, (0, 1, 3, 2, 4))
    flat_end = final_positions.reshape(IMAGES, MEMBERS, 3, ATOMS)
    flat_start = configuration.reshape(IMAGES, 3, ATOMS)
    start_centroid = jnp.sum(jnp.take(flat_start, cv_atoms, axis=2), axis=-1) / GSIZE
    moved_all = jnp.take(flat_end - flat_start[:, None], cv_atoms, axis=3)
    drift = jnp.sum(moved_all, axis=(1, 4)) / (MEMBERS * GSIZE)
    updated = start_centroid + drift
    zero_image = jnp.zeros((1, 3, NCV), jnp.float32)
    earlier = jnp.concatenate([zero_image, updated[:-1]], 0)
    later_string = jnp.concatenate([updated[1:], zero_image], 0)
    image_ids = jnp.arange(IMAGES, dtype=jnp.int32)
    neighbours = (image_ids > 0).astype(jnp.float32) + (image_ids < IMAGES - 1).astype(jnp.float32)
    new_string = updated + smoothing * (earlier + later_string - neighbours[:, None, None] * updated)
    return final_positions, new_string
```

```python
import functools

import jax
import jax.numpy as jnp
from jax import lax
from jax.experimental import pallas as pl
from jax.experimental.pallas import tpu as pltpu
from jax.sharding import PartitionSpec as P

HALO = 4096
GSIZE = 16
LANES = 128
ROWS = 8

time_step = 0.25
strength = 0.1
smoothing = 0.25

F32 = jnp.float32
BF16 = jnp.bfloat16


def three_parts(value):
    high = value.astype(BF16).astype(F32)
    rest = value - high
    middle = rest.astype(BF16).astype(F32)
    return high, middle, rest - middle


def put_rows(ref, rows):
    for place, row in enumerate(rows):
        ref[place * ROWS:(place + 1) * ROWS, :] = row


def build_group(field, rows_q, rows_v, columns, values, first):
    one, zero = jnp.ones((ROWS, LANES), F32), jnp.zeros((ROWS, LANES), F32)
    parts = [three_parts(x) for x in field]
    norm = three_parts(0.5 - 0.5 * (field[0] * field[0] + field[1] * field[1] + field[2] * field[2]))
    of_q = []
    for h, m, l in parts:
        of_q += [h, m, h, m, l, h]
    put_rows(rows_q, of_q + [one] * 3 + list(norm) + [zero] * 8)
    put_rows(
        rows_v,
        [p[0] for p in parts] + [one] + [p[2] for p in parts] + [zero]
        + [p[1] for p in parts] + [zero] * 5,
    )
    for t in range(ROWS):
        table = rows_q[pl.ds(t, 32, stride=ROWS), :]
        columns[first + t] = table.T.astype(BF16)
        values[first + t] = rows_v[pl.ds(t, 16, stride=ROWS), :].astype(BF16)


def own_rows(field, rows_p):
    one, zero = jnp.ones((ROWS, LANES), F32), jnp.zeros((ROWS, LANES), F32)
    norm = three_parts(0.5 - 0.5 * (field[0] * field[0] + field[1] * field[1] + field[2] * field[2]))
    of_p = []
    for x in field:
        h, m, l = three_parts(x)
        of_p += [h, h, m, m, h, l]
    put_rows(rows_p, of_p + list(norm) + [one] * 3 + [zero] * 8)


def group_forces(field, tile0, shift, pairs, rows_p, sums, columns, values):
    own_rows(field, rows_p)
    halo_tiles = HALO // LANES
    for t in range(ROWS):
        tile = tile0 + t
        others = [tile + halo_tiles, pairs[tile, 0], pairs[tile, 1]]
        others = [e - shift for e in others]
        p_side = rows_p[pl.ds(t, 32, stride=ROWS), :].astype(BF16)
        q_side = jnp.concatenate([columns[e] for e in others], axis=0)
        overlap = jnp.maximum(jnp.dot(q_side, p_side, preferred_element_type=F32), 0.0)
        weight = overlap * overlap
        high = weight.astype(BF16)
        low = (weight - high.astype(F32)).astype(BF16)
        q_values = jnp.concatenate([values[e] for e in others], axis=1)
        sums[t * 16:(t + 1) * 16, :] = jnp.dot(
            q_values, high, preferred_element_type=F32
        ) + jnp.dot(q_values, low, preferred_element_type=F32)
    row = lambda r: sums[pl.ds(r, ROWS, stride=16), :]
    total = row(3)
    return [
        strength * (field[c] * total - (row(c) + row(8 + c) + row(4 + c))) for c in range(3)
    ]


def inner_kernel(pairs, field_ref, out_ref, rows_q, rows_v, rows_p, sums, columns, values):
    @pl.loop(0, 16)
    def _(s):
        build_group([field_ref[s, c] for c in range(3)], rows_q, rows_v, columns, values, s * ROWS)

    @pl.loop(0, 8)
    def _(s):
        field = [field_ref[s + 4, c] for c in range(3)]
        force = group_forces(
            field, (s + 4) * ROWS, HALO // LANES, pairs, rows_p, sums, columns, values
        )
        for c in range(3):
            out_ref[s, c] = force[c]


def rim_forces(pairs, field_ref, low_ref, high_ref, rows_q, rows_v, rows_p, sums, columns, values, emit):
    for ref, first, count in ((low_ref, 0, 4), (field_ref, 4, 16), (high_ref, 20, 4)):

        @pl.loop(0, count)
        def _(s):
            build_group(
                [ref[s, c] for c in range(3)], rows_q, rows_v, columns, values, (first + s) * ROWS
            )

    @pl.loop(0, 8)
    def _(step):
        s = jnp.where(step < 4, step, step + 8)
        field = [field_ref[s, c] for c in range(3)]
        force = group_forces(field, s * ROWS, 0, pairs, rows_p, sums, columns, values)
        for c in range(3):
            emit(s, c, force[c])


def first_rim_kernel(
    pairs, field_ref, low_ref, high_ref, inner_ref, vel_ref,
    middle_ref, base_ref, rim_low_ref, rim_high_ref,
    rows_q, rows_v, rows_p, sums, columns, values,
):
    def step(s, c, force):
        velocity = vel_ref[s, c] + time_step * force
        middle = field_ref[s, c] + time_step * velocity
        middle_ref[s, c] = middle
        base_ref[s, c] = middle + time_step * velocity

    rim_forces(
        pairs, field_ref, low_ref, high_ref, rows_q, rows_v, rows_p, sums, columns, values, step
    )

    @pl.loop(0, 8)
    def _(s):
        for c in range(3):
            step(s + 4, c, inner_ref[s, c])

    rim_low_ref[...] = middle_ref[0:4]
    rim_high_ref[...] = middle_ref[12:16]


def second_rim_kernel(
    pairs, domain_ref, groups_ref, field_ref, low_ref, high_ref, inner_ref, base_ref,
    final_ref, part_ref,
    rows_q, rows_v, rows_p, sums, columns, values,
):
    def step(s, c, force):
        final_ref[c, pl.ds(pl.multiple_of(s * ROWS, ROWS), ROWS), :] = (
            base_ref[s, c] + (time_step * time_step) * force
        )

    rim_forces(
        pairs, field_ref, low_ref, high_ref, rows_q, rows_v, rows_p, sums, columns, values, step
    )

    @pl.loop(0, 8)
    def _(s):
        for c in range(3):
            step(s + 4, c, inner_ref[s, c])

    local = groups_ref[...] - domain_ref[0] * (LANES * LANES)
    tile_of, lane_of = local >> 7, local & 127
    columns_of = []
    for c in range(3):
        columns_of.append(
            jnp.concatenate([p.astype(BF16) for p in three_parts(final_ref[c].T)], axis=1)
        )
    moving = jnp.concatenate(columns_of, axis=0)
    down = lax.broadcasted_iota(jnp.int32, (LANES, LANES), 0)
    total = jnp.zeros((3 * LANES, LANES), F32)
    for g in range(GSIZE):
        chosen = (down == tile_of[g:g + 1, :]).astype(F32).astype(BF16)
        here = (down == lane_of[g:g + 1, :]).astype(F32)
        found = jnp.dot(
            moving, jnp.concatenate([chosen] * 3, axis=0), preferred_element_type=F32
        )
        total = total + found * jnp.concatenate([here] * 3, axis=0)
    zero = jnp.zeros((1, LANES), F32)
    part_ref[...] = jnp.concatenate(
        [jnp.sum(total[c * LANES:(c + 1) * LANES], axis=0, keepdims=True) for c in range(3)]
        + [zero] * 5,
        axis=0,
    )


def pack_kernel(vel_ref, conf_ref, out_ref):
    for c in range(3):
        for j in range(ROWS):
            for half in range(2):
                out_ref[pl.ds(half * 8 * 48 + c * ROWS + j, ROWS, stride=48), :] = vel_ref[
                    c, half * 8:half * 8 + 8, j * LANES:(j + 1) * LANES
                ]
        for m in range(16):
            out_ref[m * 48 + 24 + c * ROWS:m * 48 + 32 + c * ROWS, :] = conf_ref[c]


VMEM = pl.BlockSpec(memory_space=pltpu.VMEM)
SMEM = pl.BlockSpec(memory_space=pltpu.SMEM)


def scratch(tiles):
    return [
        pltpu.VMEM((32 * ROWS, LANES), F32),
        pltpu.VMEM((16 * ROWS, LANES), F32),
        pltpu.VMEM((32 * ROWS, LANES), F32),
        pltpu.VMEM((16 * ROWS, LANES), F32),
        pltpu.VMEM((tiles, LANES, 32), BF16),
        pltpu.VMEM((tiles, 16, LANES), BF16),
    ]


def call(kernel, name, out, specs, scratches, flops, moved):
    return pl.pallas_call(
        kernel,
        out_shape=out,
        in_specs=specs,
        out_specs=jax.tree.map(lambda _: VMEM, out),
        scratch_shapes=scratches,
        compiler_params=pltpu.CompilerParams(vmem_limit_bytes=40 * 1024 * 1024),
        cost_estimate=pl.CostEstimate(flops=flops, bytes_accessed=moved, transcendentals=0),
        name=name,
    )


WORK = 8_000_000_000


def shape(*dims):
    return jax.ShapeDtypeStruct(dims, F32)


def rims(low, high):
    count = lax.axis_size("domain")
    forward = [(i, i + 1) for i in range(count - 1)]
    backward = [(i + 1, i) for i in range(count - 1)]
    return lax.ppermute(high, "domain", forward), lax.ppermute(low, "domain", backward)


def on_device(configuration, velocities, pairs, cv_atoms):
    partners = pairs[0]
    groups = cv_atoms.T
    domain = lax.axis_index("domain").astype(jnp.int32).reshape(1)
    packed = call(pack_kernel, "pack", shape(16 * 48, LANES), [VMEM, VMEM], [], 0, 600_000)(
        velocities.reshape(3, 16, 1024), configuration.reshape(3, ROWS, LANES)
    )
    got = lax.all_to_all(
        packed.reshape(16, 6, ROWS, LANES), "swarm", split_axis=0, concat_axis=0, tiled=True
    )
    start_vel, start_pos = got[:, :3], got[:, 3:]

    inner = call(inner_kernel, "inner", shape(8, 3, ROWS, LANES), [SMEM, VMEM], scratch(128), WORK, 0)
    low, high = rims(start_pos[0:4], start_pos[12:16])
    inside = inner(partners, start_pos)
    whole, rim = shape(16, 3, ROWS, LANES), shape(4, 3, ROWS, LANES)
    middle, base, rim_low, rim_high = call(
        first_rim_kernel, "first_rim", (whole, whole, rim, rim), [SMEM] + [VMEM] * 5,
        scratch(192), WORK, 0,
    )(partners, start_pos, low, high, inside, start_vel)

    low, high = rims(rim_low, rim_high)
    inside = inner(partners, middle)
    final, part = call(
        second_rim_kernel, "second_rim", (shape(3, LANES, LANES), shape(ROWS, LANES)),
        [SMEM, SMEM] + [VMEM] * 6, scratch(192), WORK, 0,
    )(partners, domain, groups, middle, low, high, inside, base)
    final_positions = final.reshape(1, 1, 3, 1, LANES * LANES)

    here = part
    for offset in range(1, 4):
        here = here + lax.ppermute(part, "domain", [(i, i ^ offset) for i in range(4)])
    images, members = lax.axis_size("image"), lax.axis_size("swarm")
    everyone = lax.all_to_all(
        jnp.broadcast_to(here[None], (images * members, ROWS, LANES)),
        ("image", "swarm"), split_axis=0, concat_axis=0, tiled=True,
    )
    updated = jnp.sum(everyone.reshape(images, members, ROWS, LANES), axis=1) / (members * GSIZE)
    place = lax.axis_index("image")
    ids = jnp.arange(images)
    neighbours = (place > 0).astype(F32) + (place < images - 1).astype(F32)
    share = jnp.where(jnp.abs(ids - place) == 1, smoothing, 0.0) + jnp.where(
        ids == place, 1.0 - smoothing * neighbours, 0.0
    )
    new_string = jnp.sum(share[:, None, None] * updated, axis=0)[None, :3]
    return (final_positions, new_string)


def solution(mesh):
    in_specs = (
        P("image", None, "domain", "swarm"),
        P("image", None, "domain", None, "swarm"),
        P("domain", None, None),
        P(),
    )
    out_specs = (P("image", "swarm", None, "domain", None), P("image", None, None))
    return jax.shard_map(
        on_device, mesh=mesh, in_specs=in_specs, out_specs=out_specs, check_vma=False
    )
```

```python
import functools

import jax
import jax.numpy as jnp
from jax import lax
from jax.experimental import pallas as pl
from jax.experimental.pallas import tpu as pltpu
from jax.sharding import PartitionSpec as P

HALO = 4096
GSIZE = 16
LANES = 128
ROWS = 8

time_step = 0.25
strength = 0.1
smoothing = 0.25

F32 = jnp.float32
BF16 = jnp.bfloat16


def three_parts(value):
    high = value.astype(BF16).astype(F32)
    rest = value - high
    middle = rest.astype(BF16).astype(F32)
    return high, middle, rest - middle


def put_rows(ref, rows):
    for place, row in enumerate(rows):
        ref[place * ROWS:(place + 1) * ROWS, :] = row


def build_group(field, rows_q, rows_v, columns, values, first):
    one, zero = jnp.ones((ROWS, LANES), F32), jnp.zeros((ROWS, LANES), F32)
    parts = [three_parts(x) for x in field]
    norm = three_parts(0.5 - 0.5 * (field[0] * field[0] + field[1] * field[1] + field[2] * field[2]))
    of_q = []
    for h, m, l in parts:
        of_q += [h, m, h, m, l, h]
    put_rows(rows_q, of_q + [one] * 3 + list(norm) + [zero] * 8)
    put_rows(
        rows_v,
        [p[0] for p in parts] + [one] + [p[2] for p in parts] + [zero]
        + [p[1] for p in parts] + [zero] * 5,
    )
    for t in range(ROWS):
        columns[first + t] = rows_q[pl.ds(t, 32, stride=ROWS), :].astype(BF16)
        values[first + t] = rows_v[pl.ds(t, 16, stride=ROWS), :].astype(BF16)


def own_rows(field, rows_p):
    one, zero = jnp.ones((ROWS, LANES), F32), jnp.zeros((ROWS, LANES), F32)
    norm = three_parts(0.5 - 0.5 * (field[0] * field[0] + field[1] * field[1] + field[2] * field[2]))
    of_p = []
    for x in field:
        h, m, l = three_parts(x)
        of_p += [h, h, m, m, h, l]
    put_rows(rows_p, of_p + list(norm) + [one] * 3 + [zero] * 8)


def group_forces(field, tile0, shift, pairs, rows_p, sums, columns, values):
    own_rows(field, rows_p)
    halo_tiles = HALO // LANES
    for t in range(ROWS):
        tile = tile0 + t
        others = [tile + halo_tiles, pairs[tile, 0], pairs[tile, 1]]
        others = [e - shift for e in others]
        p_side = rows_p[pl.ds(t, 32, stride=ROWS), :].astype(BF16)
        q_side = jnp.concatenate([columns[e] for e in others], axis=1)
        overlap = jnp.maximum(
            lax.dot_general(
                q_side, p_side, (((0,), (0,)), ((), ())), preferred_element_type=F32
            ),
            0.0,
        )
        weight = overlap * overlap
        high = weight.astype(BF16)
        low = (weight - high.astype(F32)).astype(BF16)
        q_values = jnp.concatenate([values[e] for e in others], axis=1)
        sums[t * 16:(t + 1) * 16, :] = jnp.dot(
            jnp.concatenate([q_values] * 2, axis=1),
            jnp.concatenate([high, low], axis=0),
            preferred_element_type=F32,
        )
    row = lambda r: sums[pl.ds(r, ROWS, stride=16), :]
    total = row(3)
    return [
        strength * (field[c] * total - (row(c) + row(8 + c) + row(4 + c))) for c in range(3)
    ]


def inner_kernel(pairs, field_ref, out_ref, rows_q, rows_v, rows_p, sums, columns, values):
    @pl.loop(0, 16)
    def _(s):
        build_group([field_ref[s, c] for c in range(3)], rows_q, rows_v, columns, values, s * ROWS)

    for s in range(8):
        field = [field_ref[s + 4, c] for c in range(3)]
        force = group_forces(
            field, (s + 4) * ROWS, HALO // LANES, pairs, rows_p, sums, columns, values
        )
        for c in range(3):
            out_ref[s, c] = force[c]


def rim_forces(pairs, field_ref, low_ref, high_ref, rows_q, rows_v, rows_p, sums, columns, values, emit):
    for ref, first, count in ((low_ref, 0, 4), (field_ref, 4, 16), (high_ref, 20, 4)):

        @pl.loop(0, count)
        def _(s):
            build_group(
                [ref[s, c] for c in range(3)], rows_q, rows_v, columns, values, (first + s) * ROWS
            )

    for s in (0, 1, 2, 3, 12, 13, 14, 15):
        field = [field_ref[s, c] for c in range(3)]
        force = group_forces(field, s * ROWS, 0, pairs, rows_p, sums, columns, values)
        for c in range(3):
            emit(s, c, force[c])


def first_rim_kernel(
    pairs, field_ref, low_ref, high_ref, inner_ref, vel_ref,
    middle_ref, base_ref, rim_low_ref, rim_high_ref,
    rows_q, rows_v, rows_p, sums, columns, values,
):
    def step(s, c, force):
        velocity = vel_ref[s, c] + time_step * force
        middle = field_ref[s, c] + time_step * velocity
        middle_ref[s, c] = middle
        base_ref[s, c] = middle + time_step * velocity

    rim_forces(
        pairs, field_ref, low_ref, high_ref, rows_q, rows_v, rows_p, sums, columns, values, step
    )

    for s in range(8):
        for c in range(3):
            step(s + 4, c, inner_ref[s, c])

    rim_low_ref[...] = middle_ref[0:4]
    rim_high_ref[...] = middle_ref[12:16]


def second_rim_kernel(
    pairs, domain_ref, groups_ref, field_ref, low_ref, high_ref, inner_ref, base_ref,
    final_ref, part_ref,
    rows_q, rows_v, rows_p, sums, columns, values,
):
    def step(s, c, force):
        final_ref[c, pl.ds(s * ROWS, ROWS), :] = (
            base_ref[s, c] + (time_step * time_step) * force
        )

    rim_forces(
        pairs, field_ref, low_ref, high_ref, rows_q, rows_v, rows_p, sums, columns, values, step
    )

    for s in range(8):
        for c in range(3):
            step(s + 4, c, inner_ref[s, c])

    local = groups_ref[...] - domain_ref[0] * (LANES * LANES)
    tile_of, lane_of = local >> 7, local & 127
    columns_of = []
    for c in range(3):
        columns_of.append(
            jnp.concatenate([p.astype(BF16) for p in three_parts(final_ref[c].T)], axis=1)
        )
    moving = jnp.concatenate(columns_of, axis=0)
    down = lax.broadcasted_iota(jnp.int32, (LANES, LANES), 0)
    total = jnp.zeros((3 * LANES, LANES), F32)
    for g in range(GSIZE):
        chosen = (down == tile_of[g:g + 1, :]).astype(F32).astype(BF16)
        here = (down == lane_of[g:g + 1, :]).astype(F32)
        found = jnp.dot(
            moving, jnp.concatenate([chosen] * 3, axis=0), preferred_element_type=F32
        )
        total = total + found * jnp.concatenate([here] * 3, axis=0)
    for c in range(3):
        part_ref[:, c * LANES:(c + 1) * LANES] = jnp.sum(
            total[c * LANES:(c + 1) * LANES], axis=0, keepdims=True
        )


def pack_kernel(vel_ref, conf_ref, out_ref):
    for c in range(3):
        for j in range(ROWS):
            for half in range(2):
                out_ref[pl.ds(half * 8 * 48 + c * ROWS + j, ROWS, stride=48), :] = vel_ref[
                    c, half * 8:half * 8 + 8, j * LANES:(j + 1) * LANES
                ]
        for m in range(16):
            out_ref[m * 48 + 24 + c * ROWS:m * 48 + 32 + c * ROWS, :] = conf_ref[c]


VMEM = pl.BlockSpec(memory_space=pltpu.VMEM)
SMEM = pl.BlockSpec(memory_space=pltpu.SMEM)


def scratch(tiles):
    return [
        pltpu.VMEM((32 * ROWS, LANES), F32),
        pltpu.VMEM((16 * ROWS, LANES), F32),
        pltpu.VMEM((32 * ROWS, LANES), F32),
        pltpu.VMEM((16 * ROWS, LANES), F32),
        pltpu.VMEM((tiles, 32, LANES), BF16),
        pltpu.VMEM((tiles, 16, LANES), BF16),
    ]


def call(kernel, name, out, specs, scratches, flops, moved):
    return pl.pallas_call(
        kernel,
        out_shape=out,
        in_specs=specs,
        out_specs=jax.tree.map(lambda _: VMEM, out),
        scratch_shapes=scratches,
        compiler_params=pltpu.CompilerParams(vmem_limit_bytes=40 * 1024 * 1024),
        cost_estimate=pl.CostEstimate(flops=flops, bytes_accessed=moved, transcendentals=0),
        name=name,
    )


WORK = 8_000_000_000


def shape(*dims):
    return jax.ShapeDtypeStruct(dims, F32)


def rims(low, high):
    count = lax.axis_size("domain")
    forward = [(i, i + 1) for i in range(count - 1)]
    backward = [(i + 1, i) for i in range(count - 1)]
    return lax.ppermute(high, "domain", forward), lax.ppermute(low, "domain", backward)


def on_device(configuration, velocities, pairs, cv_atoms):
    partners = pairs[0]
    groups = cv_atoms.T
    domain = lax.axis_index("domain").astype(jnp.int32).reshape(1)
    packed = call(pack_kernel, "pack", shape(16 * 48, LANES), [VMEM, VMEM], [], 0, 600_000)(
        velocities.reshape(3, 16, 1024), configuration.reshape(3, ROWS, LANES)
    )
    got = lax.all_to_all(
        packed.reshape(16, 6, ROWS, LANES), "swarm", split_axis=0, concat_axis=0, tiled=True
    )
    start_vel, start_pos = got[:, :3], got[:, 3:]

    inner = call(inner_kernel, "inner", shape(8, 3, ROWS, LANES), [SMEM, VMEM], scratch(128), WORK, 0)
    low, high = rims(start_pos[0:4], start_pos[12:16])
    inside = inner(partners, start_pos)
    whole, rim = shape(16, 3, ROWS, LANES), shape(4, 3, ROWS, LANES)
    middle, base, rim_low, rim_high = call(
        first_rim_kernel, "first_rim", (whole, whole, rim, rim), [SMEM] + [VMEM] * 5,
        scratch(192), WORK, 0,
    )(partners, start_pos, low, high, inside, start_vel)

    low, high = rims(rim_low, rim_high)
    inside = inner(partners, middle)
    final, part = call(
        second_rim_kernel, "second_rim", (shape(3, LANES, LANES), shape(1, 3 * LANES)),
        [SMEM, SMEM] + [VMEM] * 6, scratch(192), WORK, 0,
    )(partners, domain, groups, middle, low, high, inside, base)
    final_positions = final.reshape(1, 1, 3, 1, LANES * LANES)

    here = part
    for offset in range(1, 4):
        here = here + lax.ppermute(part, "domain", [(i, i ^ offset) for i in range(4)])
    images, members = lax.axis_size("image"), lax.axis_size("swarm")
    everyone = lax.all_to_all(
        jnp.broadcast_to(here[None], (images * members, 1, 3 * LANES)),
        ("image", "swarm"), split_axis=0, concat_axis=0, tiled=True,
    )
    updated = jnp.sum(everyone.reshape(images, members, 3 * LANES), axis=1) / (members * GSIZE)
    place = lax.axis_index("image")
    ids = jnp.arange(images)
    neighbours = (place > 0).astype(F32) + (place < images - 1).astype(F32)
    share = jnp.where(jnp.abs(ids - place) == 1, smoothing, 0.0) + jnp.where(
        ids == place, 1.0 - smoothing * neighbours, 0.0
    )
    new_string = jnp.sum(share[:, None] * updated, axis=0).reshape(1, 3, LANES)
    return (final_positions, new_string)


def solution(mesh):
    in_specs = (
        P("image", None, "domain", "swarm"),
        P("image", None, "domain", None, "swarm"),
        P("domain", None, None),
        P(),
    )
    out_specs = (P("image", "swarm", None, "domain", None), P("image", None, None))
    return jax.shard_map(
        on_device, mesh=mesh, in_specs=in_specs, out_specs=out_specs, check_vma=False
    )
```

```python
import functools

import jax
import jax.numpy as jnp
from jax import lax
from jax.experimental import pallas as pl
from jax.experimental.pallas import tpu as pltpu
from jax.sharding import PartitionSpec as P

HALO = 4096
GSIZE = 16
LANES = 128
ROWS = 8

time_step = 0.25
strength = 0.1
smoothing = 0.25

F32 = jnp.float32
BF16 = jnp.bfloat16


def three_parts(value):
    high = value.astype(BF16).astype(F32)
    rest = value - high
    middle = rest.astype(BF16).astype(F32)
    return high, middle, rest - middle


def two_parts(value):
    high = value.astype(BF16)
    return high, (value - high.astype(F32)).astype(BF16)


def put_rows(ref, rows):
    for place, row in enumerate(rows):
        ref[place * ROWS:(place + 1) * ROWS, :] = row


def build_group(field, rows_q, rows_v, columns, values, first):
    one, zero = jnp.ones((ROWS, LANES), F32), jnp.zeros((ROWS, LANES), F32)
    parts = [three_parts(x) for x in field]
    norm = three_parts(0.5 - 0.5 * (field[0] * field[0] + field[1] * field[1] + field[2] * field[2]))
    of_q = []
    for h, m, l in parts:
        of_q += [h, m, h, m, l, h]
    put_rows(rows_q, of_q + [one] * 3 + list(norm) + [zero] * 8)
    put_rows(
        rows_v,
        [p[0] for p in parts] + [one] + [p[2] for p in parts] + [zero]
        + [p[1] for p in parts] + [zero] * 5,
    )
    for t in range(ROWS):
        columns[first + t] = rows_q[pl.ds(t, 32, stride=ROWS), :].astype(BF16)
        values[first + t] = rows_v[pl.ds(t, 16, stride=ROWS), :].astype(BF16)


def own_rows(field, rows_p):
    one, zero = jnp.ones((ROWS, LANES), F32), jnp.zeros((ROWS, LANES), F32)
    norm = three_parts(0.5 - 0.5 * (field[0] * field[0] + field[1] * field[1] + field[2] * field[2]))
    of_p = []
    for x in field:
        h, m, l = three_parts(x)
        of_p += [h, h, m, m, h, l]
    put_rows(rows_p, of_p + list(norm) + [one] * 3 + [zero] * 8)


def group_forces(field, tile0, shift, pairs, rows_p, sums, columns, values):
    own_rows(field, rows_p)
    halo_tiles = HALO // LANES
    for t in range(ROWS):
        tile = tile0 + t
        others = [tile + halo_tiles, pairs[tile, 0], pairs[tile, 1]]
        others = [e - shift for e in others]
        p_side = rows_p[pl.ds(t, 32, stride=ROWS), :].astype(BF16)
        q_side = jnp.concatenate([columns[e] for e in others], axis=1)
        overlap = jnp.maximum(
            lax.dot_general(
                q_side, p_side, (((0,), (0,)), ((), ())), preferred_element_type=F32
            ),
            0.0,
        )
        weight = overlap * overlap
        high, low = two_parts(weight)
        q_values = jnp.concatenate([values[e] for e in others], axis=1)
        sums[t * 16:(t + 1) * 16, :] = jnp.dot(
            jnp.concatenate([q_values] * 2, axis=1),
            jnp.concatenate([high, low], axis=0),
            preferred_element_type=F32,
        )
    row = lambda r: sums[pl.ds(r, ROWS, stride=16), :]
    total = row(3)
    return [
        strength * (field[c] * total - (row(c) + row(8 + c) + row(4 + c))) for c in range(3)
    ]


def inner_kernel(pairs, field_ref, out_ref, columns, values, rows_q, rows_v, rows_p, sums):
    @pl.loop(0, 16)
    def _(s):
        build_group([field_ref[s, c] for c in range(3)], rows_q, rows_v, columns, values, s * ROWS)

    for s in range(8):
        field = [field_ref[s + 4, c] for c in range(3)]
        force = group_forces(
            field, (s + 4) * ROWS, HALO // LANES, pairs, rows_p, sums, columns, values
        )
        for c in range(3):
            out_ref[s, c] = force[c]


def rim_forces(
    pairs, place, field_ref, rim_refs, own_tables, rows_q, rows_v, rows_p, sums, columns, values, emit
):
    @pl.loop(0, 16)
    def _(s):
        for whole, own in ((columns, own_tables[0]), (values, own_tables[1])):
            whole[pl.ds(HALO // LANES + s * ROWS, ROWS)] = own[pl.ds(s * ROWS, ROWS)]

    odd = place[1]
    for ref, first in ((rim_refs[0], 20 * (1 - odd)), (rim_refs[1], 20 * odd)):

        @pl.loop(0, 4)
        def _(s):
            build_group(
                [ref[s, c] for c in range(3)], rows_q, rows_v, columns, values, (first + s) * ROWS
            )

    for s in (0, 1, 2, 3, 12, 13, 14, 15):
        field = [field_ref[s, c] for c in range(3)]
        force = group_forces(field, s * ROWS, 0, pairs, rows_p, sums, columns, values)
        for c in range(3):
            emit(s, c, force[c])


def first_rim_kernel(
    pairs, place, field_ref, rim1_ref, rim2_ref, inner_ref, columns_ref, values_ref, vel_ref,
    middle_ref, base_ref, send1_ref, send2_ref,
    rows_q, rows_v, rows_p, sums, columns, values,
):
    def step(s, c, force):
        velocity = vel_ref[s, c] + time_step * force
        middle = field_ref[s, c] + time_step * velocity
        middle_ref[s, c] = middle
        base_ref[s, c] = middle + time_step * velocity

    rim_forces(
        pairs, place, field_ref, (rim1_ref, rim2_ref), (columns_ref, values_ref),
        rows_q, rows_v, rows_p, sums, columns, values, step,
    )
    for s in range(8):
        for c in range(3):
            step(s + 4, c, inner_ref[s, c])

    odd = place[1]
    send1_ref[...] = middle_ref[pl.ds(12 * (1 - odd), 4)]
    send2_ref[...] = middle_ref[pl.ds(12 * odd, 4)]


def second_rim_kernel(
    pairs, place, groups_ref, field_ref, rim1_ref, rim2_ref, inner_ref, columns_ref, values_ref,
    base_ref, final_ref, part_ref,
    rows_q, rows_v, rows_p, sums, columns, values,
):
    def step(s, c, force):
        final_ref[c, pl.ds(s * ROWS, ROWS), :] = (
            base_ref[s, c] + (time_step * time_step) * force
        )

    rim_forces(
        pairs, place, field_ref, (rim1_ref, rim2_ref), (columns_ref, values_ref),
        rows_q, rows_v, rows_p, sums, columns, values, step,
    )
    for s in range(8):
        for c in range(3):
            step(s + 4, c, inner_ref[s, c])

    local = groups_ref[...] - place[0] * (LANES * LANES)
    tile_of, lane_of = local >> 7, local & 127
    moving = jnp.concatenate(
        [jnp.concatenate(two_parts(final_ref[c].T), axis=1) for c in range(3)], axis=0
    )
    down = lax.broadcasted_iota(jnp.int32, (LANES, LANES), 0)
    total = jnp.zeros((3, ROWS, 2 * LANES), F32)
    for g in range(0, GSIZE, 2):
        pair = lambda rows: jnp.concatenate([down == rows[g + i:g + i + 1, :] for i in (0, 1)], axis=1)
        chosen = pair(tile_of).astype(F32).astype(BF16)
        here = pair(lane_of)
        found = jnp.dot(
            moving, jnp.concatenate([chosen] * 2, axis=0), preferred_element_type=F32
        )
        kept = jnp.where(jnp.concatenate([here] * 3, axis=0), found, 0.0)
        total = total + jnp.sum(kept.reshape(3, LANES // ROWS, ROWS, 2 * LANES), axis=1)
    for c in range(3):
        both = total[c, :, :LANES] + total[c, :, LANES:]
        part_ref[:, c * LANES:(c + 1) * LANES] = jnp.sum(both, axis=0, keepdims=True)


def pack_kernel(vel_hbm, conf_hbm, out_ref, vel_ref, conf_ref, arrived):
    vel_copy = pltpu.make_async_copy(vel_hbm, vel_ref, arrived.at[0])
    conf_copy = pltpu.make_async_copy(conf_hbm, conf_ref, arrived.at[1])
    vel_copy.start()
    conf_copy.start()
    conf_copy.wait()
    for c in range(3):
        for m in range(16):
            out_ref[m * 48 + 24 + c * ROWS:m * 48 + 32 + c * ROWS, :] = conf_ref[c]
    vel_copy.wait()
    for c in range(3):
        for j in range(ROWS):
            for half in range(2):
                out_ref[pl.ds(half * 8 * 48 + c * ROWS + j, ROWS, stride=48), :] = vel_ref[
                    c, half * 8:half * 8 + 8, j * LANES:(j + 1) * LANES
                ]


VMEM = pl.BlockSpec(memory_space=pltpu.VMEM)
SMEM = pl.BlockSpec(memory_space=pltpu.SMEM)
ANY = pl.BlockSpec(memory_space=pl.ANY)


ROW_SCRATCH = [
    pltpu.VMEM((32 * ROWS, LANES), F32),
    pltpu.VMEM((16 * ROWS, LANES), F32),
    pltpu.VMEM((32 * ROWS, LANES), F32),
    pltpu.VMEM((16 * ROWS, LANES), F32),
]
TABLES = [pltpu.VMEM((192, 32, LANES), BF16), pltpu.VMEM((192, 16, LANES), BF16)]


def call(kernel, name, out, specs, scratches, flops, moved, vmem=40 * 1024 * 1024):
    return pl.pallas_call(
        kernel,
        out_shape=out,
        in_specs=specs,
        out_specs=jax.tree.map(lambda _: VMEM, out),
        scratch_shapes=scratches,
        compiler_params=pltpu.CompilerParams(vmem_limit_bytes=vmem),
        cost_estimate=pl.CostEstimate(flops=flops, bytes_accessed=moved, transcendentals=0),
        name=name,
    )


WORK = 8_000_000_000


def shape(*dims):
    return jax.ShapeDtypeStruct(dims, F32)


def swap_rims(first, second):
    count = lax.axis_size("domain")
    inside = [(i, i ^ 1) for i in range(count)]
    across = [(i, j) for i in range(count) for j in [i + 1 if i % 2 else i - 1] if 0 <= j < count]
    return lax.ppermute(first, "domain", inside), lax.ppermute(second, "domain", across)


def string_shares():
    images, place = lax.axis_size("image"), lax.axis_index("image")
    ids = jnp.arange(images)
    neighbours = (place > 0).astype(F32) + (place < images - 1).astype(F32)
    return jnp.where(jnp.abs(ids - place) == 1, smoothing, 0.0) + jnp.where(
        ids == place, 1.0 - smoothing * neighbours, 0.0
    )


def on_device(configuration, velocities, pairs, cv_atoms):
    partners = pairs[0]
    groups = cv_atoms.T
    domain = lax.axis_index("domain").astype(jnp.int32)
    odd = domain % 2
    place = jnp.stack([domain, odd])
    packed = call(
        pack_kernel, "pack", shape(16 * 48, LANES), [ANY, ANY],
        [
            pltpu.VMEM((3, 16, 1024), F32),
            pltpu.VMEM((3, ROWS, LANES), F32),
            pltpu.SemaphoreType.DMA((2,)),
        ],
        0, 600_000, 62_900_000,
    )(velocities.reshape(3, 16, 1024), configuration.reshape(3, ROWS, LANES))
    got = lax.all_to_all(
        packed.reshape(16, 6, ROWS, LANES), "swarm", split_axis=0, concat_axis=0, tiled=True
    )
    start_vel, start_pos = got[:, :3], got[:, 3:]

    whole, rim = shape(16, 3, ROWS, LANES), shape(4, 3, ROWS, LANES)
    tables = (
        jax.ShapeDtypeStruct((128, 32, LANES), BF16), jax.ShapeDtypeStruct((128, 16, LANES), BF16)
    )
    inner = call(
        inner_kernel, "inner", (shape(8, 3, ROWS, LANES),) + tables, [SMEM, VMEM], ROW_SCRATCH, WORK, 0
    )
    rim1, rim2 = swap_rims(
        lax.dynamic_slice_in_dim(start_pos, 12 * (1 - odd), 4, 0),
        lax.dynamic_slice_in_dim(start_pos, 12 * odd, 4, 0),
    )
    inside = inner(partners, start_pos)
    middle, base, send1, send2 = call(
        first_rim_kernel, "first_rim", (whole, whole, rim, rim), [SMEM, SMEM] + [VMEM] * 7,
        ROW_SCRATCH + TABLES, WORK, 0,
    )(partners, place, start_pos, rim1, rim2, *inside, start_vel)

    rim1, rim2 = swap_rims(send1, send2)
    inside = inner(partners, middle)
    final, part = call(
        second_rim_kernel, "second_rim", (shape(3, LANES, LANES), shape(1, 3 * LANES)),
        [SMEM, SMEM] + [VMEM] * 8, ROW_SCRATCH + TABLES, WORK, 0,
    )(partners, place, groups, middle, rim1, rim2, *inside, base)
    part, share = lax.optimization_barrier((part, string_shares()))
    final_positions = final.reshape(1, 1, 3, 1, LANES * LANES)

    here = part
    for offset in range(1, 4):
        here = here + lax.ppermute(part, "domain", [(i, i ^ offset) for i in range(4)])
    images, members = lax.axis_size("image"), lax.axis_size("swarm")
    everyone = lax.all_to_all(
        jnp.broadcast_to(here[None], (images * members, 1, 3 * LANES)),
        ("image", "swarm"), split_axis=0, concat_axis=0, tiled=True,
    )
    updated = jnp.sum(everyone.reshape(images, members, 3 * LANES), axis=1) / (members * GSIZE)
    new_string = jnp.sum(share[:, None] * updated, axis=0).reshape(1, 3, LANES)
    return (final_positions, new_string)


def solution(mesh):
    in_specs = (
        P("image", None, "domain", "swarm"),
        P("image", None, "domain", None, "swarm"),
        P("domain", None, None),
        P(),
    )
    out_specs = (P("image", "swarm", None, "domain", None), P("image", None, None))
    return jax.shard_map(
        on_device, mesh=mesh, in_specs=in_specs, out_specs=out_specs, check_vma=False
    )
```

```python
import functools

import jax
import jax.numpy as jnp
from jax import lax
from jax.experimental import pallas as pl
from jax.experimental.pallas import tpu as pltpu
from jax.sharding import PartitionSpec as P

HALO = 4096
GSIZE = 16
LANES = 128
ROWS = 8
LAG = 5
SLOTS = 16

time_step = 0.25
strength = 0.1
smoothing = 0.25

F32 = jnp.float32
BF16 = jnp.bfloat16


def three_parts(value):
    high = value.astype(BF16).astype(F32)
    rest = value - high
    middle = rest.astype(BF16).astype(F32)
    return high, middle, rest - middle


def two_parts(value):
    high = value.astype(BF16)
    return high, (value - high.astype(F32)).astype(BF16)


def put_rows(ref, rows):
    for place, row in enumerate(rows):
        ref[place * ROWS:(place + 1) * ROWS, :] = row


def build_group(field, rows_q, rows_v, columns, values, first):
    one, zero = jnp.ones((ROWS, LANES), F32), jnp.zeros((ROWS, LANES), F32)
    parts = [three_parts(x) for x in field]
    norm = three_parts(0.5 - 0.5 * (field[0] * field[0] + field[1] * field[1] + field[2] * field[2]))
    of_q = []
    for h, m, l in parts:
        of_q += [h, m, h, m, l, h]
    put_rows(rows_q, of_q + [one] * 3 + list(norm) + [zero] * 8)
    put_rows(
        rows_v,
        [p[0] for p in parts] + [one] + [p[2] for p in parts] + [zero]
        + [p[1] for p in parts] + [zero] * 5,
    )
    for t in range(ROWS):
        columns[first + t] = rows_q[pl.ds(t, 32, stride=ROWS), :].astype(BF16)
        values[first + t] = rows_v[pl.ds(t, 16, stride=ROWS), :].astype(BF16)


def put_own_rows(field, rows_p, first):
    one, zero = jnp.ones((ROWS, LANES), F32), jnp.zeros((ROWS, LANES), F32)
    norm = three_parts(0.5 - 0.5 * (field[0] * field[0] + field[1] * field[1] + field[2] * field[2]))
    of_p = []
    for x in field:
        h, m, l = three_parts(x)
        of_p += [h, h, m, m, h, l]
    put_rows(rows_p.at[pl.ds(first, 32 * ROWS)], of_p + list(norm) + [one] * 3 + [zero] * 8)


def forces(groups, field_ref, shift, pairs, rows_p, sums, weights, columns, values, emit):
    def place_of(n):
        group, t = divmod(n, ROWS)
        tile = groups[group] * ROWS + t
        others = [tile + HALO // LANES, pairs[0, tile], pairs[1, tile]]
        return group, t, [e - shift for e in others]

    def make_weights(n):
        group, t, others = place_of(n)
        if t == 0:
            put_own_rows([field_ref[groups[group], c] for c in range(3)], rows_p, group * 32 * ROWS)
        p_side = rows_p[pl.ds(group * 32 * ROWS + t, 32, stride=ROWS), :].astype(BF16)
        q_side = jnp.concatenate([columns[e] for e in others], axis=1)
        overlap = jnp.maximum(
            lax.dot_general(
                q_side, p_side, (((0,), (0,)), ((), ())), preferred_element_type=F32
            ),
            0.0,
        )
        high, low = two_parts(overlap * overlap)
        weights[n % SLOTS, :3 * LANES] = high
        weights[n % SLOTS, 3 * LANES:] = low

    def use_weights(n):
        group, t, others = place_of(n)
        q_values = jnp.concatenate([values[e] for e in others], axis=1)
        base = group * 16 * ROWS
        sums[base + t * 16:base + (t + 1) * 16, :] = jnp.dot(
            jnp.concatenate([q_values] * 2, axis=1), weights[n % SLOTS], preferred_element_type=F32
        )
        if t == ROWS - 1:
            row = lambda r: sums[pl.ds(base + r, ROWS, stride=16), :]
            total = row(3)
            for c in range(3):
                pulled = row(c) + row(8 + c) + row(4 + c)
                emit(groups[group], c, strength * (field_ref[groups[group], c] * total - pulled))

    count = len(groups) * ROWS
    for n in range(count + LAG):
        if n < count:
            make_weights(n)
        if n >= LAG:
            use_weights(n - LAG)


def inner_kernel(pairs, field_ref, out_ref, columns, values, rows_q, rows_v, rows_p, sums, weights):
    @pl.loop(0, 16)
    def _(s):
        build_group([field_ref[s, c] for c in range(3)], rows_q, rows_v, columns, values, s * ROWS)

    def emit(s, c, force):
        out_ref[s - 4, c] = force

    forces(
        range(4, 12), field_ref, HALO // LANES, pairs, rows_p, sums, weights, columns, values, emit
    )


def rim_forces(
    pairs, place, field_ref, rim_refs, own_tables, rows_q, rows_v, rows_p, sums, weights, columns, values, emit
):
    @pl.loop(0, 16)
    def _(s):
        for whole, own in ((columns, own_tables[0]), (values, own_tables[1])):
            whole[pl.ds(HALO // LANES + s * ROWS, ROWS)] = own[pl.ds(s * ROWS, ROWS)]

    odd = place[1]
    for ref, first in ((rim_refs[0], 20 * (1 - odd)), (rim_refs[1], 20 * odd)):

        @pl.loop(0, 4)
        def _(s):
            build_group(
                [ref[s, c] for c in range(3)], rows_q, rows_v, columns, values, (first + s) * ROWS
            )

    forces(
        (0, 1, 2, 3, 12, 13, 14, 15), field_ref, 0, pairs, rows_p, sums, weights, columns, values, emit
    )


def first_rim_kernel(
    pairs, place, field_ref, rim1_ref, rim2_ref, inner_ref, columns_ref, values_ref, vel_ref,
    middle_ref, base_ref, send1_ref, send2_ref,
    rows_q, rows_v, rows_p, sums, weights, columns, values,
):
    def step(s, c, force):
        velocity = vel_ref[s, c] + time_step * force
        middle = field_ref[s, c] + time_step * velocity
        middle_ref[s, c] = middle
        base_ref[s, c] = middle + time_step * velocity

    rim_forces(
        pairs, place, field_ref, (rim1_ref, rim2_ref), (columns_ref, values_ref),
        rows_q, rows_v, rows_p, sums, weights, columns, values, step,
    )
    for s in range(8):
        for c in range(3):
            step(s + 4, c, inner_ref[s, c])

    odd = place[1]
    send1_ref[...] = middle_ref[pl.ds(12 * (1 - odd), 4)]
    send2_ref[...] = middle_ref[pl.ds(12 * odd, 4)]


def second_rim_kernel(
    pairs, place, groups_ref, field_ref, rim1_ref, rim2_ref, inner_ref, columns_ref, values_ref,
    base_ref, final_ref, part_ref,
    rows_q, rows_v, rows_p, sums, weights, columns, values,
):
    def step(s, c, force):
        final_ref[c, pl.ds(s * ROWS, ROWS), :] = (
            base_ref[s, c] + (time_step * time_step) * force
        )

    rim_forces(
        pairs, place, field_ref, (rim1_ref, rim2_ref), (columns_ref, values_ref),
        rows_q, rows_v, rows_p, sums, weights, columns, values, step,
    )
    for s in range(8):
        for c in range(3):
            step(s + 4, c, inner_ref[s, c])

    local = groups_ref[...] - place[0] * (LANES * LANES)
    tile_of, lane_of = local >> 7, local & 127
    moving = jnp.concatenate(
        [jnp.concatenate(two_parts(final_ref[c].T), axis=1) for c in range(3)], axis=0
    )
    down = lax.broadcasted_iota(jnp.int32, (LANES, LANES), 0)
    total = jnp.zeros((3, ROWS, 2 * LANES), F32)
    for g in range(0, GSIZE, 2):
        pair = lambda rows: jnp.concatenate([down == rows[g + i:g + i + 1, :] for i in (0, 1)], axis=1)
        chosen = pair(tile_of).astype(F32).astype(BF16)
        here = pair(lane_of)
        found = jnp.dot(
            moving, jnp.concatenate([chosen] * 2, axis=0), preferred_element_type=F32
        )
        kept = jnp.where(jnp.concatenate([here] * 3, axis=0), found, 0.0)
        total = total + jnp.sum(kept.reshape(3, LANES // ROWS, ROWS, 2 * LANES), axis=1)
    for c in range(3):
        both = total[c, :, :LANES] + total[c, :, LANES:]
        part_ref[:, c * LANES:(c + 1) * LANES] = jnp.sum(both, axis=0, keepdims=True)


def pack_kernel(vel_hbm, conf_hbm, out_ref, vel_ref, conf_ref, arrived):
    vel_copy = pltpu.make_async_copy(vel_hbm, vel_ref, arrived.at[0])
    conf_copy = pltpu.make_async_copy(conf_hbm, conf_ref, arrived.at[1])
    vel_copy.start()
    conf_copy.start()
    conf_copy.wait()
    for c in range(3):
        for m in range(16):
            out_ref[m * 48 + 24 + c * ROWS:m * 48 + 32 + c * ROWS, :] = conf_ref[c]
    vel_copy.wait()
    for c in range(3):
        for j in range(ROWS):
            for half in range(2):
                out_ref[pl.ds(half * 8 * 48 + c * ROWS + j, ROWS, stride=48), :] = vel_ref[
                    c, half * 8:half * 8 + 8, j * LANES:(j + 1) * LANES
                ]


VMEM = pl.BlockSpec(memory_space=pltpu.VMEM)
SMEM = pl.BlockSpec(memory_space=pltpu.SMEM)
ANY = pl.BlockSpec(memory_space=pl.ANY)


ROW_SCRATCH = [
    pltpu.VMEM((32 * ROWS, LANES), F32),
    pltpu.VMEM((16 * ROWS, LANES), F32),
    pltpu.VMEM((8 * 32 * ROWS, LANES), F32),
    pltpu.VMEM((8 * 16 * ROWS, LANES), F32),
    pltpu.VMEM((SLOTS, 6 * LANES, LANES), BF16),
]
TABLES = [pltpu.VMEM((192, 32, LANES), BF16), pltpu.VMEM((192, 16, LANES), BF16)]


def call(kernel, name, out, specs, scratches, flops, moved, vmem=40 * 1024 * 1024):
    return pl.pallas_call(
        kernel,
        out_shape=out,
        in_specs=specs,
        out_specs=jax.tree.map(lambda _: VMEM, out),
        scratch_shapes=scratches,
        compiler_params=pltpu.CompilerParams(vmem_limit_bytes=vmem),
        cost_estimate=pl.CostEstimate(flops=flops, bytes_accessed=moved, transcendentals=0),
        name=name,
    )


WORK = 8_000_000_000


def shape(*dims):
    return jax.ShapeDtypeStruct(dims, F32)


def swap_rims(first, second):
    count = lax.axis_size("domain")
    inside = [(i, i ^ 1) for i in range(count)]
    across = [(i, j) for i in range(count) for j in [i + 1 if i % 2 else i - 1] if 0 <= j < count]
    return lax.ppermute(first, "domain", inside), lax.ppermute(second, "domain", across)


def string_shares(place):
    images = lax.axis_size("image")
    ids = jnp.arange(images)
    neighbours = (place > 0).astype(F32) + (place < images - 1).astype(F32)
    return jnp.where(jnp.abs(ids - place) == 1, smoothing, 0.0) + jnp.where(
        ids == place, 1.0 - smoothing * neighbours, 0.0
    )


def on_device(configuration, velocities, pairs, cv_atoms):
    partners = pairs[0].T
    groups = cv_atoms.T
    configuration, velocities, domain, image = lax.optimization_barrier(
        (configuration, velocities, lax.axis_index("domain"), lax.axis_index("image"))
    )
    packed = call(
        pack_kernel, "pack", shape(16 * 48, LANES), [ANY, ANY],
        [
            pltpu.VMEM((3, 16, 1024), F32),
            pltpu.VMEM((3, ROWS, LANES), F32),
            pltpu.SemaphoreType.DMA((2,)),
        ],
        0, 600_000, 62_900_000,
    )(velocities.reshape(3, 16, 1024), configuration.reshape(3, ROWS, LANES))
    got = lax.all_to_all(
        packed.reshape(16, 6, ROWS, LANES), "swarm", split_axis=0, concat_axis=0, tiled=True
    )
    got, domain, image = lax.optimization_barrier((got, domain, image))
    start_vel, start_pos = got[:, :3], got[:, 3:]
    odd = domain % 2
    place = jnp.stack([domain, odd])

    whole, rim = shape(16, 3, ROWS, LANES), shape(4, 3, ROWS, LANES)
    tables = (
        jax.ShapeDtypeStruct((128, 32, LANES), BF16), jax.ShapeDtypeStruct((128, 16, LANES), BF16)
    )
    inner = call(
        inner_kernel, "inner", (shape(8, 3, ROWS, LANES),) + tables, [SMEM, VMEM], ROW_SCRATCH, WORK, 0
    )
    rim1, rim2 = swap_rims(
        lax.dynamic_slice_in_dim(start_pos, 12 * (1 - odd), 4, 0),
        lax.dynamic_slice_in_dim(start_pos, 12 * odd, 4, 0),
    )
    inside = inner(partners, start_pos)
    middle, base, send1, send2 = call(
        first_rim_kernel, "first_rim", (whole, whole, rim, rim), [SMEM, SMEM] + [VMEM] * 7,
        ROW_SCRATCH + TABLES, WORK, 0,
    )(partners, place, start_pos, rim1, rim2, *inside, start_vel)

    rim1, rim2 = swap_rims(send1, send2)
    inside = inner(partners, middle)
    final, part = call(
        second_rim_kernel, "second_rim", (shape(3, LANES, LANES), shape(1, 3 * LANES)),
        [SMEM, SMEM] + [VMEM] * 8, ROW_SCRATCH + TABLES, WORK, 0,
    )(partners, place, groups, middle, rim1, rim2, *inside, base)
    images, members = lax.axis_size("image"), lax.axis_size("swarm")
    shares = jnp.broadcast_to(
        (string_shares(image) / (members * GSIZE))[:, None], (images, 3 * LANES)
    )
    part, shares = lax.optimization_barrier((part, shares))
    final_positions = final.reshape(1, 1, 3, 1, LANES * LANES)

    here = part
    for offset in range(1, 4):
        here = here + lax.ppermute(part, "domain", [(i, i ^ offset) for i in range(4)])
    everyone = lax.all_to_all(
        jnp.broadcast_to(here[None], (images * members, 1, 3 * LANES)),
        ("image", "swarm"), split_axis=0, concat_axis=0, tiled=True,
    )
    mixed = everyone.reshape(images, members, 3 * LANES) * shares[:, None]
    new_string = jnp.sum(mixed, axis=(0, 1)).reshape(1, 3, LANES)
    return (final_positions, new_string)


def solution(mesh):
    in_specs = (
        P("image", None, "domain", "swarm"),
        P("image", None, "domain", None, "swarm"),
        P("domain", None, None),
        P(),
    )
    out_specs = (P("image", "swarm", None, "domain", None), P("image", None, None))
    return jax.shard_map(
        on_device, mesh=mesh, in_specs=in_specs, out_specs=out_specs, check_vma=False
    )
```

```python
import functools

import jax
import jax.numpy as jnp
from jax import lax
from jax.experimental import pallas as pl
from jax.experimental.pallas import tpu as pltpu
from jax.sharding import PartitionSpec as P

HALO = 4096
GSIZE = 16
LANES = 128
ROWS = 8
LAG = 5
SLOTS = 16

time_step = 0.25
strength = 0.1
smoothing = 0.25

F32 = jnp.float32
BF16 = jnp.bfloat16


def three_parts(value):
    high = value.astype(BF16).astype(F32)
    rest = value - high
    middle = rest.astype(BF16).astype(F32)
    return high, middle, rest - middle


def two_parts(value):
    high = value.astype(BF16)
    return high, (value - high.astype(F32)).astype(BF16)


def put_rows(ref, rows):
    for place, row in enumerate(rows):
        ref[place * ROWS:(place + 1) * ROWS, :] = row


def build_group(field, rows_q, rows_v, columns, values, first):
    one, zero = jnp.ones((ROWS, LANES), F32), jnp.zeros((ROWS, LANES), F32)
    parts = [three_parts(x) for x in field]
    norm = three_parts(0.5 - 0.5 * (field[0] * field[0] + field[1] * field[1] + field[2] * field[2]))
    of_q = []
    for h, m, l in parts:
        of_q += [h, m, h, m, l, h]
    put_rows(rows_q, of_q + [one] * 3 + list(norm) + [zero] * 8)
    put_rows(
        rows_v,
        [p[0] for p in parts] + [one] + [p[2] for p in parts] + [zero]
        + [p[1] for p in parts] + [zero] * 5,
    )
    for t in range(ROWS):
        columns[first + t] = rows_q[pl.ds(t, 32, stride=ROWS), :].astype(BF16)
        values[first + t] = rows_v[pl.ds(t, 16, stride=ROWS), :].astype(BF16)


def put_own_rows(field, rows_p, first):
    one, zero = jnp.ones((ROWS, LANES), F32), jnp.zeros((ROWS, LANES), F32)
    norm = three_parts(0.5 - 0.5 * (field[0] * field[0] + field[1] * field[1] + field[2] * field[2]))
    of_p = []
    for x in field:
        h, m, l = three_parts(x)
        of_p += [h, h, m, m, h, l]
    put_rows(rows_p.at[pl.ds(first, 32 * ROWS)], of_p + list(norm) + [one] * 3 + [zero] * 8)


def forces(groups, field_ref, shift, pairs, rows_p, sums, weights, columns, values, emit):
    def place_of(n):
        group, t = divmod(n, ROWS)
        tile = groups[group] * ROWS + t
        others = [tile + HALO // LANES, pairs[0, tile], pairs[1, tile]]
        return group, t, [e - shift for e in others]

    def make_weights(n):
        group, t, others = place_of(n)
        if t == 0:
            put_own_rows([field_ref[groups[group], c] for c in range(3)], rows_p, group * 32 * ROWS)
        p_side = rows_p[pl.ds(group * 32 * ROWS + t, 32, stride=ROWS), :].astype(BF16)
        q_side = jnp.concatenate([columns[e] for e in others], axis=1)
        overlap = jnp.maximum(
            lax.dot_general(
                q_side, p_side, (((0,), (0,)), ((), ())), preferred_element_type=F32
            ),
            0.0,
        )
        high, low = two_parts(overlap * overlap)
        weights[n % SLOTS, :3 * LANES] = high
        weights[n % SLOTS, 3 * LANES:] = low

    def use_weights(n):
        group, t, others = place_of(n)
        q_values = jnp.concatenate([values[e] for e in others], axis=1)
        base = group * 16 * ROWS
        sums[base + t * 16:base + (t + 1) * 16, :] = jnp.dot(
            jnp.concatenate([q_values] * 2, axis=1), weights[n % SLOTS], preferred_element_type=F32
        )
        if t == ROWS - 1:
            row = lambda r: sums[pl.ds(base + r, ROWS, stride=16), :]
            total = row(3)
            for c in range(3):
                pulled = row(c) + row(8 + c) + row(4 + c)
                emit(groups[group], c, strength * (field_ref[groups[group], c] * total - pulled))

    count = len(groups) * ROWS
    for n in range(count + LAG):
        if n < count:
            make_weights(n)
        if n >= LAG:
            use_weights(n - LAG)


def inner_kernel(pairs, field_ref, groups_ref, out_ref, columns, values, rows_q, rows_v, rows_p, sums, weights):
    @pl.loop(0, 16)
    def _(s):
        build_group([field_ref[s, c] for c in range(3)], rows_q, rows_v, columns, values, s * ROWS)

    def emit(s, c, force):
        out_ref[s - 4, c] = force

    forces(
        range(4, 12), field_ref, HALO // LANES, pairs, rows_p, sums, weights, columns, values, emit
    )


def rim_forces(
    pairs, place, field_ref, rim_refs, own_tables, rows_q, rows_v, rows_p, sums, weights, columns, values, emit
):
    @pl.loop(0, 16)
    def _(s):
        for whole, own in ((columns, own_tables[0]), (values, own_tables[1])):
            whole[pl.ds(HALO // LANES + s * ROWS, ROWS)] = own[pl.ds(s * ROWS, ROWS)]

    odd = place[1]
    for ref, first in ((rim_refs[0], 20 * (1 - odd)), (rim_refs[1], 20 * odd)):

        @pl.loop(0, 4)
        def _(s):
            build_group(
                [ref[s, c] for c in range(3)], rows_q, rows_v, columns, values, (first + s) * ROWS
            )

    forces(
        (0, 1, 2, 3, 12, 13, 14, 15), field_ref, 0, pairs, rows_p, sums, weights, columns, values, emit
    )


def first_rim_kernel(
    pairs, place, field_ref, rim1_ref, rim2_ref, inner_ref, columns_ref, values_ref, vel_ref,
    middle_ref, base_ref, send1_ref, send2_ref,
    rows_q, rows_v, rows_p, sums, weights, columns, values,
):
    def step(s, c, force):
        velocity = vel_ref[s, c] + time_step * force
        middle = field_ref[s, c] + time_step * velocity
        middle_ref[s, c] = middle
        base_ref[s, c] = middle + time_step * velocity

    rim_forces(
        pairs, place, field_ref, (rim1_ref, rim2_ref), (columns_ref, values_ref),
        rows_q, rows_v, rows_p, sums, weights, columns, values, step,
    )
    for s in range(8):
        for c in range(3):
            step(s + 4, c, inner_ref[s, c])

    odd = place[1]
    send1_ref[...] = middle_ref[pl.ds(12 * (1 - odd), 4)]
    send2_ref[...] = middle_ref[pl.ds(12 * odd, 4)]


def second_rim_kernel(
    pairs, place, groups_ref, field_ref, rim1_ref, rim2_ref, inner_ref, columns_ref, values_ref,
    base_ref, final_ref, part_ref,
    rows_q, rows_v, rows_p, sums, weights, columns, values,
):
    def step(s, c, force):
        final_ref[c, pl.ds(s * ROWS, ROWS), :] = (
            base_ref[s, c] + (time_step * time_step) * force
        )

    rim_forces(
        pairs, place, field_ref, (rim1_ref, rim2_ref), (columns_ref, values_ref),
        rows_q, rows_v, rows_p, sums, weights, columns, values, step,
    )
    for s in range(8):
        for c in range(3):
            step(s + 4, c, inner_ref[s, c])

    local = groups_ref[...] - place[0] * (LANES * LANES)
    tile_of, lane_of = local >> 7, local & 127
    moving = jnp.concatenate(
        [jnp.concatenate(two_parts(final_ref[c].T), axis=1) for c in range(3)], axis=0
    )
    down = lax.broadcasted_iota(jnp.int32, (LANES, LANES), 0)
    total = jnp.zeros((3, ROWS, 2 * LANES), F32)
    for g in range(0, GSIZE, 2):
        pair = lambda rows: jnp.concatenate([down == rows[g + i:g + i + 1, :] for i in (0, 1)], axis=1)
        chosen = pair(tile_of).astype(F32).astype(BF16)
        here = pair(lane_of)
        found = jnp.dot(
            moving, jnp.concatenate([chosen] * 2, axis=0), preferred_element_type=F32
        )
        kept = jnp.where(jnp.concatenate([here] * 3, axis=0), found, 0.0)
        total = total + jnp.sum(kept.reshape(3, LANES // ROWS, ROWS, 2 * LANES), axis=1)
    for c in range(3):
        both = total[c, :, :LANES] + total[c, :, LANES:]
        part_ref[:, c * LANES:(c + 1) * LANES] = jnp.sum(both, axis=0, keepdims=True)


def spread_kernel(own_ref, *refs):
    others, out_ref = refs[:-1], refs[-1]
    total = own_ref[...]
    for ref in others:
        total = total + ref[...]
    out_ref[...] = jnp.broadcast_to(total[None], out_ref.shape)


def string_kernel(shares, everyone_ref, out_ref):
    images = shares.shape[0]
    members = everyone_ref.shape[0] // images
    total = jnp.zeros((1, 3 * LANES), F32)
    for i in range(images):
        updated = jnp.sum(everyone_ref[i * members:(i + 1) * members], axis=0)
        total = total + shares[i] * updated
    for c in range(3):
        out_ref[c] = total[:, c * LANES:(c + 1) * LANES]


def pack_kernel(vel_hbm, conf_hbm, out_ref, vel_ref, conf_ref, arrived):
    vel_copy = pltpu.make_async_copy(vel_hbm, vel_ref, arrived.at[0])
    conf_copy = pltpu.make_async_copy(conf_hbm, conf_ref, arrived.at[1])
    vel_copy.start()
    conf_copy.start()
    conf_copy.wait()
    for c in range(3):
        for m in range(16):
            out_ref[m * 48 + 24 + c * ROWS:m * 48 + 32 + c * ROWS, :] = conf_ref[c]
    vel_copy.wait()
    for c in range(3):
        for j in range(ROWS):
            for half in range(2):
                out_ref[pl.ds(half * 8 * 48 + c * ROWS + j, ROWS, stride=48), :] = vel_ref[
                    c, half * 8:half * 8 + 8, j * LANES:(j + 1) * LANES
                ]


VMEM = pl.BlockSpec(memory_space=pltpu.VMEM)
SMEM = pl.BlockSpec(memory_space=pltpu.SMEM)
ANY = pl.BlockSpec(memory_space=pl.ANY)


ROW_SCRATCH = [
    pltpu.VMEM((32 * ROWS, LANES), F32),
    pltpu.VMEM((16 * ROWS, LANES), F32),
    pltpu.VMEM((8 * 32 * ROWS, LANES), F32),
    pltpu.VMEM((8 * 16 * ROWS, LANES), F32),
    pltpu.VMEM((SLOTS, 6 * LANES, LANES), BF16),
]
TABLES = [pltpu.VMEM((192, 32, LANES), BF16), pltpu.VMEM((192, 16, LANES), BF16)]


def call(kernel, name, out, specs, scratches, flops, moved, vmem=40 * 1024 * 1024):
    return pl.pallas_call(
        kernel,
        out_shape=out,
        in_specs=specs,
        out_specs=jax.tree.map(lambda _: VMEM, out),
        scratch_shapes=scratches,
        compiler_params=pltpu.CompilerParams(vmem_limit_bytes=vmem),
        cost_estimate=pl.CostEstimate(flops=flops, bytes_accessed=moved, transcendentals=0),
        name=name,
    )


WORK = 8_000_000_000


def shape(*dims):
    return jax.ShapeDtypeStruct(dims, F32)


def swap_rims(first, second):
    count = lax.axis_size("domain")
    inside = [(i, i ^ 1) for i in range(count)]
    across = [(i, j) for i in range(count) for j in [i + 1 if i % 2 else i - 1] if 0 <= j < count]
    return lax.ppermute(first, "domain", inside), lax.ppermute(second, "domain", across)


def string_shares(place):
    images = lax.axis_size("image")
    ids = jnp.arange(images)
    neighbours = (place > 0).astype(F32) + (place < images - 1).astype(F32)
    return jnp.where(jnp.abs(ids - place) == 1, smoothing, 0.0) + jnp.where(
        ids == place, 1.0 - smoothing * neighbours, 0.0
    )


def on_device(configuration, velocities, pairs, cv_atoms):
    partners = pairs[0].T
    groups = cv_atoms.T
    configuration, velocities, domain, image = lax.optimization_barrier(
        (configuration, velocities, lax.axis_index("domain"), lax.axis_index("image"))
    )
    packed = call(
        pack_kernel, "pack", shape(16 * 48, LANES), [ANY, ANY],
        [
            pltpu.VMEM((3, 16, 1024), F32),
            pltpu.VMEM((3, ROWS, LANES), F32),
            pltpu.SemaphoreType.DMA((2,)),
        ],
        0, 600_000, 62_900_000,
    )(velocities.reshape(3, 16, 1024), configuration.reshape(3, ROWS, LANES))
    got = lax.all_to_all(
        packed.reshape(16, 6, ROWS, LANES), "swarm", split_axis=0, concat_axis=0, tiled=True
    )
    got, domain, image = lax.optimization_barrier((got, domain, image))
    start_vel, start_pos = got[:, :3], got[:, 3:]
    odd = domain % 2
    place = jnp.stack([domain, odd])

    whole, rim = shape(16, 3, ROWS, LANES), shape(4, 3, ROWS, LANES)
    tables = (
        jax.ShapeDtypeStruct((128, 32, LANES), BF16), jax.ShapeDtypeStruct((128, 16, LANES), BF16)
    )
    inner = call(
        inner_kernel, "inner", (shape(8, 3, ROWS, LANES),) + tables, [SMEM, VMEM, VMEM], ROW_SCRATCH, WORK, 0
    )
    rim1, rim2 = swap_rims(
        lax.dynamic_slice_in_dim(start_pos, 12 * (1 - odd), 4, 0),
        lax.dynamic_slice_in_dim(start_pos, 12 * odd, 4, 0),
    )
    inside = inner(partners, start_pos, groups)
    middle, base, send1, send2 = call(
        first_rim_kernel, "first_rim", (whole, whole, rim, rim), [SMEM, SMEM] + [VMEM] * 7,
        ROW_SCRATCH + TABLES, WORK, 0,
    )(partners, place, start_pos, rim1, rim2, *inside, start_vel)

    rim1, rim2 = swap_rims(send1, send2)
    inside = inner(partners, middle, groups)
    final, part = call(
        second_rim_kernel, "second_rim", (shape(3, LANES, LANES), shape(1, 3 * LANES)),
        [SMEM, SMEM] + [VMEM] * 8, ROW_SCRATCH + TABLES, WORK, 0,
    )(partners, place, groups, middle, rim1, rim2, *inside, base)
    images, members = lax.axis_size("image"), lax.axis_size("swarm")
    shares = string_shares(image) / (members * GSIZE)
    part, shares = lax.optimization_barrier((part, shares))
    final_positions = final.reshape(1, 1, 3, 1, LANES * LANES)

    parts = [part] + [
        lax.ppermute(part, "domain", [(i, i ^ offset) for i in range(4)]) for offset in (1, 2, 3)
    ]
    copies = call(
        spread_kernel, "spread", shape(images * members, 1, 3 * LANES), [VMEM] * 4, [], 0, 100_000
    )(*parts)
    everyone = lax.all_to_all(copies, ("image", "swarm"), split_axis=0, concat_axis=0, tiled=True)
    new_string = call(
        string_kernel, "string", shape(3, 1, LANES), [SMEM, VMEM], [], 0, 100_000
    )(shares, everyone)
    new_string = new_string.transpose(1, 0, 2)
    return (final_positions, new_string)


def solution(mesh):
    in_specs = (
        P("image", None, "domain", "swarm"),
        P("image", None, "domain", None, "swarm"),
        P("domain", None, None),
        P(),
    )
    out_specs = (P("image", "swarm", None, "domain", None), P("image", None, None))
    return jax.shard_map(
        on_device, mesh=mesh, in_specs=in_specs, out_specs=out_specs, check_vma=False
    )
```

```python
import functools

import jax
import jax.numpy as jnp
from jax import lax
from jax.experimental import pallas as pl
from jax.experimental.pallas import tpu as pltpu
from jax.sharding import PartitionSpec as P

HALO = 4096
GSIZE = 16
LANES = 128
ROWS = 8
LAG = 5
SLOTS = 16

time_step = 0.25
strength = 0.1
smoothing = 0.25

F32 = jnp.float32
BF16 = jnp.bfloat16


def three_parts(value):
    high = value.astype(BF16).astype(F32)
    rest = value - high
    middle = rest.astype(BF16).astype(F32)
    return high, middle, rest - middle


def two_parts(value):
    high = value.astype(BF16)
    return high, (value - high.astype(F32)).astype(BF16)


def put_rows(ref, rows):
    for place, row in enumerate(rows):
        ref[place * ROWS:(place + 1) * ROWS, :] = row


def build_group(field, rows_q, rows_v, columns, values, first):
    one, zero = jnp.ones((ROWS, LANES), F32), jnp.zeros((ROWS, LANES), F32)
    parts = [three_parts(x) for x in field]
    norm = three_parts(0.5 - 0.5 * (field[0] * field[0] + field[1] * field[1] + field[2] * field[2]))
    of_q = []
    for h, m, l in parts:
        of_q += [h, m, h, m, l, h]
    put_rows(rows_q, of_q + [one] * 3 + list(norm) + [zero] * 8)
    put_rows(
        rows_v,
        [p[0] for p in parts] + [one] + [p[2] for p in parts] + [zero]
        + [p[1] for p in parts] + [zero] * 5,
    )
    for t in range(ROWS):
        columns[first + t] = rows_q[pl.ds(t, 32, stride=ROWS), :].astype(BF16)
        values[first + t] = rows_v[pl.ds(t, 16, stride=ROWS), :].astype(BF16)


def put_own_rows(field, rows_p, first):
    one, zero = jnp.ones((ROWS, LANES), F32), jnp.zeros((ROWS, LANES), F32)
    norm = three_parts(0.5 - 0.5 * (field[0] * field[0] + field[1] * field[1] + field[2] * field[2]))
    of_p = []
    for x in field:
        h, m, l = three_parts(x)
        of_p += [h, h, m, m, h, l]
    put_rows(rows_p.at[pl.ds(first, 32 * ROWS)], of_p + list(norm) + [one] * 3 + [zero] * 8)


def forces(groups, field_ref, shift, pairs, rows_p, sums, weights, columns, values, emit):
    def place_of(n):
        group, t = divmod(n, ROWS)
        tile = groups[group] * ROWS + t
        others = [tile + HALO // LANES, pairs[0, tile], pairs[1, tile]]
        return group, t, [e - shift for e in others]

    def make_weights(n):
        group, t, others = place_of(n)
        if t == 0:
            put_own_rows([field_ref[groups[group], c] for c in range(3)], rows_p, group * 32 * ROWS)
        p_side = rows_p[pl.ds(group * 32 * ROWS + t, 32, stride=ROWS), :].astype(BF16)
        q_side = jnp.concatenate([columns[e] for e in others], axis=1)
        overlap = jnp.maximum(
            lax.dot_general(
                q_side, p_side, (((0,), (0,)), ((), ())), preferred_element_type=F32
            ),
            0.0,
        )
        high, low = two_parts(overlap * overlap)
        weights[n % SLOTS, :3 * LANES] = high
        weights[n % SLOTS, 3 * LANES:] = low

    def use_weights(n):
        group, t, others = place_of(n)
        q_values = jnp.concatenate([values[e] for e in others], axis=1)
        base = group * 16 * ROWS
        sums[base + t * 16:base + (t + 1) * 16, :] = jnp.dot(
            jnp.concatenate([q_values] * 2, axis=1), weights[n % SLOTS], preferred_element_type=F32
        )
        if t == ROWS - 1:
            row = lambda r: sums[pl.ds(base + r, ROWS, stride=16), :]
            total = row(3)
            for c in range(3):
                pulled = row(c) + row(8 + c) + row(4 + c)
                emit(groups[group], c, strength * (field_ref[groups[group], c] * total - pulled))

    count = len(groups) * ROWS
    for n in range(count + LAG):
        if n < count:
            make_weights(n)
        if n >= LAG:
            use_weights(n - LAG)


def inner_kernel(pairs, field_ref, out_ref, columns, values, rows_q, rows_v, rows_p, sums, weights):
    @pl.loop(0, 16)
    def _(s):
        build_group([field_ref[s, c] for c in range(3)], rows_q, rows_v, columns, values, s * ROWS)

    def emit(s, c, force):
        out_ref[s - 4, c] = force

    forces(
        range(4, 12), field_ref, HALO // LANES, pairs, rows_p, sums, weights, columns, values, emit
    )


def rim_forces(
    pairs, place, field_ref, rim_refs, own_tables, rows_q, rows_v, rows_p, sums, weights, columns, values, emit
):
    @pl.loop(0, 16)
    def _(s):
        for whole, own in ((columns, own_tables[0]), (values, own_tables[1])):
            whole[pl.ds(HALO // LANES + s * ROWS, ROWS)] = own[pl.ds(s * ROWS, ROWS)]

    odd = place[1]
    for ref, first in ((rim_refs[0], 20 * (1 - odd)), (rim_refs[1], 20 * odd)):

        @pl.loop(0, 4)
        def _(s):
            build_group(
                [ref[s, c] for c in range(3)], rows_q, rows_v, columns, values, (first + s) * ROWS
            )

    forces(
        (0, 1, 2, 3, 12, 13, 14, 15), field_ref, 0, pairs, rows_p, sums, weights, columns, values, emit
    )


def first_rim_kernel(
    pairs, place, field_ref, rim1_ref, rim2_ref, inner_ref, columns_ref, values_ref, vel_ref,
    middle_ref, base_ref, send1_ref, send2_ref,
    rows_q, rows_v, rows_p, sums, weights, columns, values,
):
    def step(s, c, force):
        velocity = vel_ref[s, c] + time_step * force
        middle = field_ref[s, c] + time_step * velocity
        middle_ref[s, c] = middle
        base_ref[s, c] = middle + time_step * velocity

    rim_forces(
        pairs, place, field_ref, (rim1_ref, rim2_ref), (columns_ref, values_ref),
        rows_q, rows_v, rows_p, sums, weights, columns, values, step,
    )
    for s in range(8):
        for c in range(3):
            step(s + 4, c, inner_ref[s, c])

    odd = place[1]
    send1_ref[...] = middle_ref[pl.ds(12 * (1 - odd), 4)]
    send2_ref[...] = middle_ref[pl.ds(12 * odd, 4)]


def second_rim_kernel(
    pairs, place, groups_ref, field_ref, rim1_ref, rim2_ref, inner_ref, columns_ref, values_ref,
    base_ref, final_ref, part_ref,
    rows_q, rows_v, rows_p, sums, weights, columns, values,
):
    def step(s, c, force):
        final_ref[c, pl.ds(s * ROWS, ROWS), :] = (
            base_ref[s, c] + (time_step * time_step) * force
        )

    rim_forces(
        pairs, place, field_ref, (rim1_ref, rim2_ref), (columns_ref, values_ref),
        rows_q, rows_v, rows_p, sums, weights, columns, values, step,
    )
    for s in range(8):
        for c in range(3):
            step(s + 4, c, inner_ref[s, c])

    local = groups_ref[...] - place[0] * (LANES * LANES)
    tile_of, lane_of = local >> 7, local & 127
    moving = jnp.concatenate(
        [jnp.concatenate(two_parts(final_ref[c].T), axis=1) for c in range(3)], axis=0
    )
    down = lax.broadcasted_iota(jnp.int32, (LANES, LANES), 0)
    total = jnp.zeros((3, ROWS, 2 * LANES), F32)
    for g in range(0, GSIZE, 2):
        pair = lambda rows: jnp.concatenate([down == rows[g + i:g + i + 1, :] for i in (0, 1)], axis=1)
        chosen = pair(tile_of).astype(F32).astype(BF16)
        here = pair(lane_of)
        found = jnp.dot(
            moving, jnp.concatenate([chosen] * 2, axis=0), preferred_element_type=F32
        )
        kept = jnp.where(jnp.concatenate([here] * 3, axis=0), found, 0.0)
        total = total + jnp.sum(kept.reshape(3, LANES // ROWS, ROWS, 2 * LANES), axis=1)
    for c in range(3):
        both = total[c, :, :LANES] + total[c, :, LANES:]
        part_ref[:, c * LANES:(c + 1) * LANES] = jnp.sum(both, axis=0, keepdims=True)


def fetch_kernel(pairs_ref, groups_ref, pairs_out, groups_out):
    pairs_out[...] = pairs_ref[...]
    groups_out[...] = groups_ref[...]


def spread_kernel(own_ref, *refs):
    others, out_ref = refs[:-1], refs[-1]
    total = own_ref[...]
    for ref in others:
        total = total + ref[...]
    out_ref[...] = jnp.broadcast_to(total[None], out_ref.shape)


def pack_kernel(vel_hbm, conf_hbm, out_ref, vel_ref, conf_ref, arrived):
    vel_copy = pltpu.make_async_copy(vel_hbm, vel_ref, arrived.at[0])
    conf_copy = pltpu.make_async_copy(conf_hbm, conf_ref, arrived.at[1])
    vel_copy.start()
    conf_copy.start()
    conf_copy.wait()
    for c in range(3):
        for m in range(16):
            out_ref[m * 48 + 24 + c * ROWS:m * 48 + 32 + c * ROWS, :] = conf_ref[c]
    vel_copy.wait()
    for c in range(3):
        for j in range(ROWS):
            for half in range(2):
                out_ref[pl.ds(half * 8 * 48 + c * ROWS + j, ROWS, stride=48), :] = vel_ref[
                    c, half * 8:half * 8 + 8, j * LANES:(j + 1) * LANES
                ]


VMEM = pl.BlockSpec(memory_space=pltpu.VMEM)
SMEM = pl.BlockSpec(memory_space=pltpu.SMEM)
ANY = pl.BlockSpec(memory_space=pl.ANY)


ROW_SCRATCH = [
    pltpu.VMEM((32 * ROWS, LANES), F32),
    pltpu.VMEM((16 * ROWS, LANES), F32),
    pltpu.VMEM((8 * 32 * ROWS, LANES), F32),
    pltpu.VMEM((8 * 16 * ROWS, LANES), F32),
    pltpu.VMEM((SLOTS, 6 * LANES, LANES), BF16),
]
TABLES = [pltpu.VMEM((192, 32, LANES), BF16), pltpu.VMEM((192, 16, LANES), BF16)]


def call(kernel, name, out, specs, scratches, flops, moved, vmem=40 * 1024 * 1024):
    return pl.pallas_call(
        kernel,
        out_shape=out,
        in_specs=specs,
        out_specs=jax.tree.map(lambda _: VMEM, out),
        scratch_shapes=scratches,
        compiler_params=pltpu.CompilerParams(vmem_limit_bytes=vmem),
        cost_estimate=pl.CostEstimate(flops=flops, bytes_accessed=moved, transcendentals=0),
        name=name,
    )


WORK = 8_000_000_000


def shape(*dims):
    return jax.ShapeDtypeStruct(dims, F32)


def swap_rims(first, second):
    count = lax.axis_size("domain")
    inside = [(i, i ^ 1) for i in range(count)]
    across = [(i, j) for i in range(count) for j in [i + 1 if i % 2 else i - 1] if 0 <= j < count]
    return lax.ppermute(first, "domain", inside), lax.ppermute(second, "domain", across)


def string_shares(place):
    images = lax.axis_size("image")
    ids = jnp.arange(images)
    neighbours = (place > 0).astype(F32) + (place < images - 1).astype(F32)
    return jnp.where(jnp.abs(ids - place) == 1, smoothing, 0.0) + jnp.where(
        ids == place, 1.0 - smoothing * neighbours, 0.0
    )


def on_device(configuration, velocities, pairs, cv_atoms):
    partners = pairs[0].T
    groups = cv_atoms.T
    configuration, velocities, domain, image = lax.optimization_barrier(
        (configuration, velocities, lax.axis_index("domain"), lax.axis_index("image"))
    )
    packed = call(
        pack_kernel, "pack", shape(16 * 48, LANES), [ANY, ANY],
        [
            pltpu.VMEM((3, 16, 1024), F32),
            pltpu.VMEM((3, ROWS, LANES), F32),
            pltpu.SemaphoreType.DMA((2,)),
        ],
        0, 600_000, 62_900_000,
    )(velocities.reshape(3, 16, 1024), configuration.reshape(3, ROWS, LANES))
    got = lax.all_to_all(
        packed.reshape(16, 6, ROWS, LANES), "swarm", split_axis=0, concat_axis=0, tiled=True
    )
    partners, groups = call(
        fetch_kernel, "fetch",
        (jax.ShapeDtypeStruct((2, LANES), jnp.int32), jax.ShapeDtypeStruct((GSIZE, LANES), jnp.int32)),
        [VMEM, VMEM], [], 0, 20_000,
    )(partners, groups)
    got, domain, image, partners, groups = lax.optimization_barrier(
        (got, domain, image, partners, groups)
    )
    start_vel, start_pos = got[:, :3], got[:, 3:]
    odd = domain % 2
    place = jnp.stack([domain, odd])

    whole, rim = shape(16, 3, ROWS, LANES), shape(4, 3, ROWS, LANES)
    tables = (
        jax.ShapeDtypeStruct((128, 32, LANES), BF16), jax.ShapeDtypeStruct((128, 16, LANES), BF16)
    )
    inner = call(
        inner_kernel, "inner", (shape(8, 3, ROWS, LANES),) + tables, [SMEM, VMEM], ROW_SCRATCH, WORK, 0
    )
    rim1, rim2 = swap_rims(
        lax.dynamic_slice_in_dim(start_pos, 12 * (1 - odd), 4, 0),
        lax.dynamic_slice_in_dim(start_pos, 12 * odd, 4, 0),
    )
    inside = inner(partners, start_pos)
    middle, base, send1, send2 = call(
        first_rim_kernel, "first_rim", (whole, whole, rim, rim), [SMEM, SMEM] + [VMEM] * 7,
        ROW_SCRATCH + TABLES, WORK, 0,
    )(partners, place, start_pos, rim1, rim2, *inside, start_vel)

    rim1, rim2 = swap_rims(send1, send2)
    inside = inner(partners, middle)
    final, part = call(
        second_rim_kernel, "second_rim", (shape(3, LANES, LANES), shape(1, 3 * LANES)),
        [SMEM, SMEM] + [VMEM] * 8, ROW_SCRATCH + TABLES, WORK, 0,
    )(partners, place, groups, middle, rim1, rim2, *inside, base)
    images, members = lax.axis_size("image"), lax.axis_size("swarm")
    shares = string_shares(image) / (members * GSIZE)
    part, shares = lax.optimization_barrier((part, shares))
    final_positions = final.reshape(1, 1, 3, 1, LANES * LANES)

    parts = [part] + [
        lax.ppermute(part, "domain", [(i, i ^ offset) for i in range(4)]) for offset in (1, 2, 3)
    ]
    copies = call(
        spread_kernel, "spread", shape(images * members, 1, 3 * LANES), [VMEM] * 4, [], 0, 100_000
    )(*parts)
    everyone = lax.all_to_all(copies, ("image", "swarm"), split_axis=0, concat_axis=0, tiled=True)
    updated = jnp.sum(everyone.reshape(images, members, 3 * LANES), axis=1)
    new_string = jnp.sum(shares[:, None] * updated, axis=0).reshape(1, 3, LANES)
    return (final_positions, new_string)


def solution(mesh):
    in_specs = (
        P("image", None, "domain", "swarm"),
        P("image", None, "domain", None, "swarm"),
        P("domain", None, None),
        P(),
    )
    out_specs = (P("image", "swarm", None, "domain", None), P("image", None, None))
    return jax.shard_map(
        on_device, mesh=mesh, in_specs=in_specs, out_specs=out_specs, check_vma=False
    )
```

```python
import functools

import jax
import jax.numpy as jnp
from jax import lax
from jax.experimental import pallas as pl
from jax.experimental.pallas import tpu as pltpu
from jax.sharding import PartitionSpec as P

HALO = 4096
GSIZE = 16
LANES = 128
ROWS = 8
LAG = 5
SLOTS = 16

time_step = 0.25
strength = 0.1
smoothing = 0.25

F32 = jnp.float32
BF16 = jnp.bfloat16


def three_parts(value):
    high = value.astype(BF16).astype(F32)
    rest = value - high
    middle = rest.astype(BF16).astype(F32)
    return high, middle, rest - middle


def two_parts(value):
    high = value.astype(BF16)
    return high, (value - high.astype(F32)).astype(BF16)


def put_rows(ref, rows):
    for place, row in enumerate(rows):
        ref[place * ROWS:(place + 1) * ROWS, :] = row


def build_group(field, rows_q, rows_v, columns, values, first):
    one, zero = jnp.ones((ROWS, LANES), F32), jnp.zeros((ROWS, LANES), F32)
    parts = [three_parts(x) for x in field]
    norm = three_parts(0.5 - 0.5 * (field[0] * field[0] + field[1] * field[1] + field[2] * field[2]))
    of_q = []
    for h, m, l in parts:
        of_q += [h, m, h, m, l, h]
    put_rows(rows_q, of_q + [one] * 3 + list(norm) + [zero] * 8)
    put_rows(
        rows_v,
        [p[0] for p in parts] + [one] + [p[2] for p in parts] + [zero]
        + [p[1] for p in parts] + [zero] * 5,
    )
    for t in range(ROWS):
        columns[first + t] = rows_q[pl.ds(t, 32, stride=ROWS), :].astype(BF16)
        values[first + t] = rows_v[pl.ds(t, 16, stride=ROWS), :].astype(BF16)


def put_own_rows(field, rows_p, first):
    one, zero = jnp.ones((ROWS, LANES), F32), jnp.zeros((ROWS, LANES), F32)
    norm = three_parts(0.5 - 0.5 * (field[0] * field[0] + field[1] * field[1] + field[2] * field[2]))
    of_p = []
    for x in field:
        h, m, l = three_parts(x)
        of_p += [h, h, m, m, h, l]
    put_rows(rows_p.at[pl.ds(first, 32 * ROWS)], of_p + list(norm) + [one] * 3 + [zero] * 8)


def forces(groups, field_ref, shift, pairs, rows_p, sums, weights, columns, values, emit):
    def place_of(n):
        group, t = divmod(n, ROWS)
        tile = groups[group] * ROWS + t
        others = [tile + HALO // LANES, pairs[0, tile], pairs[1, tile]]
        return group, t, [e - shift for e in others]

    def make_weights(n):
        group, t, others = place_of(n)
        if t == 0:
            put_own_rows([field_ref[groups[group], c] for c in range(3)], rows_p, group * 32 * ROWS)
        p_side = rows_p[pl.ds(group * 32 * ROWS + t, 32, stride=ROWS), :].astype(BF16)
        q_side = jnp.concatenate([columns[e] for e in others], axis=1)
        overlap = jnp.maximum(
            lax.dot_general(
                q_side, p_side, (((0,), (0,)), ((), ())), preferred_element_type=F32
            ),
            0.0,
        )
        high, low = two_parts(overlap * overlap)
        weights[n % SLOTS, :3 * LANES] = high
        weights[n % SLOTS, 3 * LANES:] = low

    def use_weights(n):
        group, t, others = place_of(n)
        q_values = jnp.concatenate([values[e] for e in others], axis=1)
        base = group * 16 * ROWS
        sums[base + t * 16:base + (t + 1) * 16, :] = jnp.dot(
            jnp.concatenate([q_values] * 2, axis=1), weights[n % SLOTS], preferred_element_type=F32
        )
        if t == ROWS - 1:
            row = lambda r: sums[pl.ds(base + r, ROWS, stride=16), :]
            total = row(3)
            for c in range(3):
                pulled = row(c) + row(8 + c) + row(4 + c)
                emit(groups[group], c, strength * (field_ref[groups[group], c] * total - pulled))

    count = len(groups) * ROWS
    for n in range(count + LAG):
        if n < count:
            make_weights(n)
        if n >= LAG:
            use_weights(n - LAG)


def inner_kernel(pairs, field_ref, out_ref, columns, values, rows_q, rows_v, rows_p, sums, weights):
    @pl.loop(0, 16)
    def _(s):
        build_group([field_ref[s, c] for c in range(3)], rows_q, rows_v, columns, values, s * ROWS)

    def emit(s, c, force):
        out_ref[s - 4, c] = force

    forces(
        range(4, 12), field_ref, HALO // LANES, pairs, rows_p, sums, weights, columns, values, emit
    )


def rim_forces(
    pairs, place, field_ref, rim_refs, own_tables, rows_q, rows_v, rows_p, sums, weights, columns, values, emit
):
    @pl.loop(0, 16)
    def _(s):
        for whole, own in ((columns, own_tables[0]), (values, own_tables[1])):
            whole[pl.ds(HALO // LANES + s * ROWS, ROWS)] = own[pl.ds(s * ROWS, ROWS)]

    odd, second = place[1], place[2] > 0
    for ref, first, exists in ((rim_refs[0], 20 * (1 - odd), None), (rim_refs[1], 20 * odd, second)):

        @pl.loop(0, 4)
        def _(s):
            field = [ref[s, c] for c in range(3)]
            if exists is not None:
                field = [jnp.where(exists, x, 0.0) for x in field]
            build_group(field, rows_q, rows_v, columns, values, (first + s) * ROWS)

    forces(
        (0, 1, 2, 3, 12, 13, 14, 15), field_ref, 0, pairs, rows_p, sums, weights, columns, values, emit
    )


def first_rim_kernel(
    pairs, place, field_ref, rim1_ref, rim2_ref, inner_ref, columns_ref, values_ref, vel_ref,
    middle_ref, base_ref, send1_ref, send2_ref,
    rows_q, rows_v, rows_p, sums, weights, columns, values,
):
    def step(s, c, force):
        velocity = vel_ref[s, c] + time_step * force
        middle = field_ref[s, c] + time_step * velocity
        middle_ref[s, c] = middle
        base_ref[s, c] = middle + time_step * velocity

    rim_forces(
        pairs, place, field_ref, (rim1_ref, rim2_ref), (columns_ref, values_ref),
        rows_q, rows_v, rows_p, sums, weights, columns, values, step,
    )
    for s in range(8):
        for c in range(3):
            step(s + 4, c, inner_ref[s, c])

    odd = place[1]
    send1_ref[...] = middle_ref[pl.ds(12 * (1 - odd), 4)]
    send2_ref[...] = middle_ref[pl.ds(12 * odd, 4)]


def second_rim_kernel(
    pairs, place, groups_ref, field_ref, rim1_ref, rim2_ref, inner_ref, columns_ref, values_ref,
    base_ref, final_ref, part_ref,
    rows_q, rows_v, rows_p, sums, weights, columns, values,
):
    def step(s, c, force):
        final_ref[c, pl.ds(s * ROWS, ROWS), :] = (
            base_ref[s, c] + (time_step * time_step) * force
        )

    rim_forces(
        pairs, place, field_ref, (rim1_ref, rim2_ref), (columns_ref, values_ref),
        rows_q, rows_v, rows_p, sums, weights, columns, values, step,
    )
    for s in range(8):
        for c in range(3):
            step(s + 4, c, inner_ref[s, c])

    local = groups_ref[...] - place[0] * (LANES * LANES)
    tile_of, lane_of = local >> 7, local & 127
    moving = jnp.concatenate(
        [jnp.concatenate(two_parts(final_ref[c].T), axis=1) for c in range(3)], axis=0
    )
    down = lax.broadcasted_iota(jnp.int32, (LANES, LANES), 0)
    total = jnp.zeros((3, ROWS, 2 * LANES), F32)
    for g in range(0, GSIZE, 2):
        pair = lambda rows: jnp.concatenate([down == rows[g + i:g + i + 1, :] for i in (0, 1)], axis=1)
        chosen = pair(tile_of).astype(F32).astype(BF16)
        here = pair(lane_of)
        found = jnp.dot(
            moving, jnp.concatenate([chosen] * 2, axis=0), preferred_element_type=F32
        )
        kept = jnp.where(jnp.concatenate([here] * 3, axis=0), found, 0.0)
        total = total + jnp.sum(kept.reshape(3, LANES // ROWS, ROWS, 2 * LANES), axis=1)
    for c in range(3):
        both = total[c, :, :LANES] + total[c, :, LANES:]
        part_ref[:, c * LANES:(c + 1) * LANES] = jnp.sum(both, axis=0, keepdims=True)


def fetch_kernel(pairs_ref, groups_ref, pairs_out, groups_out):
    pairs_out[...] = pairs_ref[...]
    groups_out[...] = groups_ref[...]


def spread_kernel(own_ref, *refs):
    others, out_ref = refs[:-1], refs[-1]
    total = own_ref[...]
    for ref in others:
        total = total + ref[...]
    out_ref[...] = jnp.broadcast_to(total[None], out_ref.shape)


def pack_kernel(vel_hbm, conf_hbm, out_ref, vel_ref, conf_ref, arrived):
    vel_copy = pltpu.make_async_copy(vel_hbm, vel_ref, arrived.at[0])
    conf_copy = pltpu.make_async_copy(conf_hbm, conf_ref, arrived.at[1])
    vel_copy.start()
    conf_copy.start()
    conf_copy.wait()
    for c in range(3):
        for m in range(16):
            out_ref[m * 48 + 24 + c * ROWS:m * 48 + 32 + c * ROWS, :] = conf_ref[c]
    vel_copy.wait()
    for c in range(3):
        for j in range(ROWS):
            for half in range(2):
                out_ref[pl.ds(half * 8 * 48 + c * ROWS + j, ROWS, stride=48), :] = vel_ref[
                    c, half * 8:half * 8 + 8, j * LANES:(j + 1) * LANES
                ]


VMEM = pl.BlockSpec(memory_space=pltpu.VMEM)
SMEM = pl.BlockSpec(memory_space=pltpu.SMEM)
ANY = pl.BlockSpec(memory_space=pl.ANY)


ROW_SCRATCH = [
    pltpu.VMEM((32 * ROWS, LANES), F32),
    pltpu.VMEM((16 * ROWS, LANES), F32),
    pltpu.VMEM((8 * 32 * ROWS, LANES), F32),
    pltpu.VMEM((8 * 16 * ROWS, LANES), F32),
    pltpu.VMEM((SLOTS, 6 * LANES, LANES), BF16),
]
TABLES = [pltpu.VMEM((192, 32, LANES), BF16), pltpu.VMEM((192, 16, LANES), BF16)]


def call(kernel, name, out, specs, scratches, flops, moved, vmem=40 * 1024 * 1024):
    return pl.pallas_call(
        kernel,
        out_shape=out,
        in_specs=specs,
        out_specs=jax.tree.map(lambda _: VMEM, out),
        scratch_shapes=scratches,
        compiler_params=pltpu.CompilerParams(vmem_limit_bytes=vmem),
        cost_estimate=pl.CostEstimate(flops=flops, bytes_accessed=moved, transcendentals=0),
        name=name,
    )


WORK = 8_000_000_000


def shape(*dims):
    return jax.ShapeDtypeStruct(dims, F32)


def swap_rims(first, second):
    count = lax.axis_size("domain")
    inside = [(i, i ^ 1) for i in range(count)]
    across = [(i, (i + 1 if i % 2 else i - 1) % count) for i in range(count)]
    return lax.ppermute(first, "domain", inside), lax.ppermute(second, "domain", across)


def string_shares(place):
    images = lax.axis_size("image")
    ids = jnp.arange(images)
    neighbours = (place > 0).astype(F32) + (place < images - 1).astype(F32)
    return jnp.where(jnp.abs(ids - place) == 1, smoothing, 0.0) + jnp.where(
        ids == place, 1.0 - smoothing * neighbours, 0.0
    )


def on_device(configuration, velocities, pairs, cv_atoms):
    partners = pairs[0].T
    groups = cv_atoms.T
    configuration, velocities, domain, image = lax.optimization_barrier(
        (configuration, velocities, lax.axis_index("domain"), lax.axis_index("image"))
    )
    packed = call(
        pack_kernel, "pack", shape(16 * 48, LANES), [ANY, ANY],
        [
            pltpu.VMEM((3, 16, 1024), F32),
            pltpu.VMEM((3, ROWS, LANES), F32),
            pltpu.SemaphoreType.DMA((2,)),
        ],
        0, 600_000, 62_900_000,
    )(velocities.reshape(3, 16, 1024), configuration.reshape(3, ROWS, LANES))
    got = lax.all_to_all(
        packed.reshape(16, 6, ROWS, LANES), "swarm", split_axis=0, concat_axis=0, tiled=True
    )
    partners, groups = call(
        fetch_kernel, "fetch",
        (jax.ShapeDtypeStruct((2, LANES), jnp.int32), jax.ShapeDtypeStruct((GSIZE, LANES), jnp.int32)),
        [VMEM, VMEM], [], 0, 20_000,
    )(partners, groups)
    got, domain, image, partners, groups = lax.optimization_barrier(
        (got, domain, image, partners, groups)
    )
    start_vel, start_pos = got[:, :3], got[:, 3:]
    odd = domain % 2
    inner_domain = (domain > 0) & (domain < lax.axis_size("domain") - 1)
    place = jnp.stack([domain, odd, inner_domain.astype(domain.dtype)])

    whole, rim = shape(16, 3, ROWS, LANES), shape(4, 3, ROWS, LANES)
    tables = (
        jax.ShapeDtypeStruct((128, 32, LANES), BF16), jax.ShapeDtypeStruct((128, 16, LANES), BF16)
    )
    inner = call(
        inner_kernel, "inner", (shape(8, 3, ROWS, LANES),) + tables, [SMEM, VMEM], ROW_SCRATCH, WORK, 0
    )
    rim1, rim2 = swap_rims(
        lax.dynamic_slice_in_dim(start_pos, 12 * (1 - odd), 4, 0),
        lax.dynamic_slice_in_dim(start_pos, 12 * odd, 4, 0),
    )
    inside = inner(partners, start_pos)
    middle, base, send1, send2 = call(
        first_rim_kernel, "first_rim", (whole, whole, rim, rim), [SMEM, SMEM] + [VMEM] * 7,
        ROW_SCRATCH + TABLES, WORK, 0,
    )(partners, place, start_pos, rim1, rim2, *inside, start_vel)

    rim1, rim2 = swap_rims(send1, send2)
    inside = inner(partners, middle)
    final, part = call(
        second_rim_kernel, "second_rim", (shape(3, LANES, LANES), shape(1, 3 * LANES)),
        [SMEM, SMEM] + [VMEM] * 8, ROW_SCRATCH + TABLES, WORK, 0,
    )(partners, place, groups, middle, rim1, rim2, *inside, base)
    images, members = lax.axis_size("image"), lax.axis_size("swarm")
    shares = string_shares(image) / (members * GSIZE)
    part, shares = lax.optimization_barrier((part, shares))
    final_positions = final.reshape(1, 1, 3, 1, LANES * LANES)

    parts = [part] + [
        lax.ppermute(part, "domain", [(i, i ^ offset) for i in range(4)]) for offset in (1, 2, 3)
    ]
    copies = call(
        spread_kernel, "spread", shape(images * members, 1, 3 * LANES), [VMEM] * 4, [], 0, 100_000
    )(*parts)
    everyone = lax.all_to_all(copies, ("image", "swarm"), split_axis=0, concat_axis=0, tiled=True)
    updated = jnp.sum(everyone.reshape(images, members, 3 * LANES), axis=1)
    new_string = jnp.sum(shares[:, None] * updated, axis=0).reshape(1, 3, LANES)
    return (final_positions, new_string)


def solution(mesh):
    in_specs = (
        P("image", None, "domain", "swarm"),
        P("image", None, "domain", None, "swarm"),
        P("domain", None, None),
        P(),
    )
    out_specs = (P("image", "swarm", None, "domain", None), P("image", None, None))
    return jax.shard_map(
        on_device, mesh=mesh, in_specs=in_specs, out_specs=out_specs, check_vma=False
    )
```

```python
import functools

import jax
import jax.numpy as jnp
from jax import lax
from jax.experimental import pallas as pl
from jax.experimental.pallas import tpu as pltpu
from jax.sharding import PartitionSpec as P

HALO = 4096
GSIZE = 16
LANES = 128
ROWS = 8
LAG = 5
SLOTS = 16

time_step = 0.25
strength = 0.1
smoothing = 0.25

F32 = jnp.float32
BF16 = jnp.bfloat16


def three_parts(value):
    high = value.astype(BF16).astype(F32)
    rest = value - high
    middle = rest.astype(BF16).astype(F32)
    return high, middle, rest - middle


def two_parts(value):
    high = value.astype(BF16)
    return high, (value - high.astype(F32)).astype(BF16)


def put_rows(ref, rows):
    for place, row in enumerate(rows):
        ref[place * ROWS:(place + 1) * ROWS, :] = row


def build_group(field, rows_q, rows_v, columns, values, first):
    one, zero = jnp.ones((ROWS, LANES), F32), jnp.zeros((ROWS, LANES), F32)
    parts = [three_parts(x) for x in field]
    norm = three_parts(0.5 - 0.5 * (field[0] * field[0] + field[1] * field[1] + field[2] * field[2]))
    of_q = []
    for h, m, l in parts:
        of_q += [h, m, h, m, l, h]
    put_rows(rows_q, of_q + [one] * 3 + list(norm) + [zero] * 8)
    put_rows(
        rows_v,
        [p[0] for p in parts] + [one] + [p[2] for p in parts] + [zero]
        + [p[1] for p in parts] + [zero] * 5,
    )
    for t in range(ROWS):
        columns[first + t] = rows_q[pl.ds(t, 32, stride=ROWS), :].astype(BF16)
        values[first + t] = rows_v[pl.ds(t, 16, stride=ROWS), :].astype(BF16)


def put_own_rows(field, rows_p, first):
    one, zero = jnp.ones((ROWS, LANES), F32), jnp.zeros((ROWS, LANES), F32)
    norm = three_parts(0.5 - 0.5 * (field[0] * field[0] + field[1] * field[1] + field[2] * field[2]))
    of_p = []
    for x in field:
        h, m, l = three_parts(x)
        of_p += [h, h, m, m, h, l]
    put_rows(rows_p.at[pl.ds(first, 32 * ROWS)], of_p + list(norm) + [one] * 3 + [zero] * 8)


def forces(groups, field_ref, shift, pairs, rows_p, sums, weights, columns, values, emit):
    def place_of(n):
        group, t = divmod(n, ROWS)
        tile = groups[group] * ROWS + t
        others = [tile + HALO // LANES, pairs[0, tile], pairs[1, tile]]
        return group, t, [e - shift for e in others]

    def make_weights(n):
        group, t, others = place_of(n)
        if t == 0:
            put_own_rows([field_ref[groups[group], c] for c in range(3)], rows_p, group * 32 * ROWS)
        p_side = rows_p[pl.ds(group * 32 * ROWS + t, 32, stride=ROWS), :].astype(BF16)
        q_side = jnp.concatenate([columns[e] for e in others], axis=1)
        overlap = jnp.maximum(
            lax.dot_general(
                q_side, p_side, (((0,), (0,)), ((), ())), preferred_element_type=F32
            ),
            0.0,
        )
        high, low = two_parts(overlap * overlap)
        weights[n % SLOTS, :3 * LANES] = high
        weights[n % SLOTS, 3 * LANES:] = low

    def use_weights(n):
        group, t, others = place_of(n)
        q_values = jnp.concatenate([values[e] for e in others], axis=1)
        base = group * 16 * ROWS
        sums[base + t * 16:base + (t + 1) * 16, :] = jnp.dot(
            jnp.concatenate([q_values] * 2, axis=1), weights[n % SLOTS], preferred_element_type=F32
        )
        if t == ROWS - 1:
            row = lambda r: sums[pl.ds(base + r, ROWS, stride=16), :]
            total = row(3)
            for c in range(3):
                pulled = row(c) + row(8 + c) + row(4 + c)
                emit(groups[group], c, strength * (field_ref[groups[group], c] * total - pulled))

    count = len(groups) * ROWS
    for n in range(count + LAG):
        if n < count:
            make_weights(n)
        if n >= LAG:
            use_weights(n - LAG)


def inner_kernel(pairs, field_ref, out_ref, columns, values, rows_q, rows_v, rows_p, sums, weights):
    @pl.loop(0, 16)
    def _(s):
        build_group([field_ref[s, c] for c in range(3)], rows_q, rows_v, columns, values, s * ROWS)

    def emit(s, c, force):
        out_ref[s - 4, c] = force

    forces(
        range(4, 12), field_ref, HALO // LANES, pairs, rows_p, sums, weights, columns, values, emit
    )


def rim_forces(
    pairs, place, field_ref, rim_refs, own_tables, rows_q, rows_v, rows_p, sums, weights, columns, values, emit
):
    @pl.loop(0, 16)
    def _(s):
        for whole, own in ((columns, own_tables[0]), (values, own_tables[1])):
            whole[pl.ds(HALO // LANES + s * ROWS, ROWS)] = own[pl.ds(s * ROWS, ROWS)]

    odd, second = place[1], place[2] > 0
    for ref, first, exists in ((rim_refs[0], 20 * (1 - odd), None), (rim_refs[1], 20 * odd, second)):

        @pl.loop(0, 4)
        def _(s):
            field = [ref[s, c] for c in range(3)]
            if exists is not None:
                field = [jnp.where(exists, x, 0.0) for x in field]
            build_group(field, rows_q, rows_v, columns, values, (first + s) * ROWS)

    forces(
        (0, 1, 2, 3, 12, 13, 14, 15), field_ref, 0, pairs, rows_p, sums, weights, columns, values, emit
    )


def first_rim_kernel(
    pairs, place, field_ref, rim1_ref, rim2_ref, inner_ref, columns_ref, values_ref, vel_ref,
    middle_ref, base_ref, send1_ref, send2_ref,
    rows_q, rows_v, rows_p, sums, weights, columns, values,
):
    def step(s, c, force):
        velocity = vel_ref[s, c] + time_step * force
        middle = field_ref[s, c] + time_step * velocity
        middle_ref[s, c] = middle
        base_ref[s, c] = middle + time_step * velocity

    rim_forces(
        pairs, place, field_ref, (rim1_ref, rim2_ref), (columns_ref, values_ref),
        rows_q, rows_v, rows_p, sums, weights, columns, values, step,
    )
    for s in range(8):
        for c in range(3):
            step(s + 4, c, inner_ref[s, c])

    odd = place[1]
    send1_ref[...] = middle_ref[pl.ds(12 * (1 - odd), 4)]
    send2_ref[...] = middle_ref[pl.ds(12 * odd, 4)]


def second_rim_kernel(
    pairs, place, groups_ref, field_ref, rim1_ref, rim2_ref, inner_ref, columns_ref, values_ref,
    base_ref, final_ref, part_ref,
    rows_q, rows_v, rows_p, sums, weights, columns, values,
):
    def step(s, c, force):
        final_ref[c, pl.ds(s * ROWS, ROWS), :] = (
            base_ref[s, c] + (time_step * time_step) * force
        )

    rim_forces(
        pairs, place, field_ref, (rim1_ref, rim2_ref), (columns_ref, values_ref),
        rows_q, rows_v, rows_p, sums, weights, columns, values, step,
    )
    for s in range(8):
        for c in range(3):
            step(s + 4, c, inner_ref[s, c])

    local = groups_ref[...] - place[0] * (LANES * LANES)
    tile_of, lane_of = local >> 7, local & 127
    moving = jnp.concatenate(
        [jnp.concatenate(two_parts(final_ref[c].T), axis=1) for c in range(3)], axis=0
    )
    down = lax.broadcasted_iota(jnp.int32, (LANES, LANES), 0)
    total = jnp.zeros((3, ROWS, 2 * LANES), F32)
    for g in range(0, GSIZE, 2):
        pair = lambda rows: jnp.concatenate([down == rows[g + i:g + i + 1, :] for i in (0, 1)], axis=1)
        chosen = pair(tile_of).astype(F32).astype(BF16)
        here = pair(lane_of)
        found = jnp.dot(
            moving, jnp.concatenate([chosen] * 2, axis=0), preferred_element_type=F32
        )
        kept = jnp.where(jnp.concatenate([here] * 3, axis=0), found, 0.0)
        total = total + jnp.sum(kept.reshape(3, LANES // ROWS, ROWS, 2 * LANES), axis=1)
    for c in range(3):
        both = total[c, :, :LANES] + total[c, :, LANES:]
        part_ref[:, c * LANES:(c + 1) * LANES] = jnp.sum(both, axis=0, keepdims=True)


def fetch_kernel(pairs_ref, groups_ref, pairs_out, groups_out):
    pairs_out[...] = pairs_ref[...]
    groups_out[...] = groups_ref[...]


def spread_kernel(own_ref, out_ref):
    out_ref[...] = jnp.broadcast_to(own_ref[...][None], out_ref.shape)


def pack_kernel(vel_hbm, conf_hbm, out_ref, vel_ref, conf_ref, arrived):
    vel_copy = pltpu.make_async_copy(vel_hbm, vel_ref, arrived.at[0])
    conf_copy = pltpu.make_async_copy(conf_hbm, conf_ref, arrived.at[1])
    vel_copy.start()
    conf_copy.start()
    conf_copy.wait()
    for c in range(3):
        for m in range(16):
            out_ref[m * 48 + 24 + c * ROWS:m * 48 + 32 + c * ROWS, :] = conf_ref[c]
    vel_copy.wait()
    for c in range(3):
        for j in range(ROWS):
            for half in range(2):
                out_ref[pl.ds(half * 8 * 48 + c * ROWS + j, ROWS, stride=48), :] = vel_ref[
                    c, half * 8:half * 8 + 8, j * LANES:(j + 1) * LANES
                ]


VMEM = pl.BlockSpec(memory_space=pltpu.VMEM)
SMEM = pl.BlockSpec(memory_space=pltpu.SMEM)
ANY = pl.BlockSpec(memory_space=pl.ANY)


ROW_SCRATCH = [
    pltpu.VMEM((32 * ROWS, LANES), F32),
    pltpu.VMEM((16 * ROWS, LANES), F32),
    pltpu.VMEM((8 * 32 * ROWS, LANES), F32),
    pltpu.VMEM((8 * 16 * ROWS, LANES), F32),
    pltpu.VMEM((SLOTS, 6 * LANES, LANES), BF16),
]
TABLES = [pltpu.VMEM((192, 32, LANES), BF16), pltpu.VMEM((192, 16, LANES), BF16)]


def call(kernel, name, out, specs, scratches, flops, moved, vmem=40 * 1024 * 1024):
    return pl.pallas_call(
        kernel,
        out_shape=out,
        in_specs=specs,
        out_specs=jax.tree.map(lambda _: VMEM, out),
        scratch_shapes=scratches,
        compiler_params=pltpu.CompilerParams(vmem_limit_bytes=vmem),
        cost_estimate=pl.CostEstimate(flops=flops, bytes_accessed=moved, transcendentals=0),
        name=name,
    )


WORK = 8_000_000_000


def shape(*dims):
    return jax.ShapeDtypeStruct(dims, F32)


def swap_rims(first, second):
    count = lax.axis_size("domain")
    inside = [(i, i ^ 1) for i in range(count)]
    across = [(i, (i + 1 if i % 2 else i - 1) % count) for i in range(count)]
    return lax.ppermute(first, "domain", inside), lax.ppermute(second, "domain", across)


def string_shares(place):
    before = (place > 0).astype(F32) * smoothing
    after = (place < lax.axis_size("image") - 1).astype(F32) * smoothing
    return jnp.stack([1.0 - before - after, before, after])


def on_device(configuration, velocities, pairs, cv_atoms):
    partners = pairs[0].T
    groups = cv_atoms.T
    configuration, velocities, domain, image = lax.optimization_barrier(
        (configuration, velocities, lax.axis_index("domain"), lax.axis_index("image"))
    )
    packed = call(
        pack_kernel, "pack", shape(16 * 48, LANES), [ANY, ANY],
        [
            pltpu.VMEM((3, 16, 1024), F32),
            pltpu.VMEM((3, ROWS, LANES), F32),
            pltpu.SemaphoreType.DMA((2,)),
        ],
        0, 600_000, 62_900_000,
    )(velocities.reshape(3, 16, 1024), configuration.reshape(3, ROWS, LANES))
    got = lax.all_to_all(
        packed.reshape(16, 6, ROWS, LANES), "swarm", split_axis=0, concat_axis=0, tiled=True
    )
    partners, groups = call(
        fetch_kernel, "fetch",
        (jax.ShapeDtypeStruct((2, LANES), jnp.int32), jax.ShapeDtypeStruct((GSIZE, LANES), jnp.int32)),
        [VMEM, VMEM], [], 0, 20_000,
    )(partners, groups)
    got, domain, image, partners, groups = lax.optimization_barrier(
        (got, domain, image, partners, groups)
    )
    start_vel, start_pos = got[:, :3], got[:, 3:]
    odd = domain % 2
    inner_domain = (domain > 0) & (domain < lax.axis_size("domain") - 1)
    place = jnp.stack([domain, odd, inner_domain.astype(domain.dtype)])

    whole, rim = shape(16, 3, ROWS, LANES), shape(4, 3, ROWS, LANES)
    tables = (
        jax.ShapeDtypeStruct((128, 32, LANES), BF16), jax.ShapeDtypeStruct((128, 16, LANES), BF16)
    )
    inner = call(
        inner_kernel, "inner", (shape(8, 3, ROWS, LANES),) + tables, [SMEM, VMEM], ROW_SCRATCH, WORK, 0
    )
    rim1, rim2 = swap_rims(
        lax.dynamic_slice_in_dim(start_pos, 12 * (1 - odd), 4, 0),
        lax.dynamic_slice_in_dim(start_pos, 12 * odd, 4, 0),
    )
    inside = inner(partners, start_pos)
    middle, base, send1, send2 = call(
        first_rim_kernel, "first_rim", (whole, whole, rim, rim), [SMEM, SMEM] + [VMEM] * 7,
        ROW_SCRATCH + TABLES, WORK, 0,
    )(partners, place, start_pos, rim1, rim2, *inside, start_vel)

    rim1, rim2 = swap_rims(send1, send2)
    inside = inner(partners, middle)
    final, part = call(
        second_rim_kernel, "second_rim", (shape(3, LANES, LANES), shape(1, 3 * LANES)),
        [SMEM, SMEM] + [VMEM] * 8, ROW_SCRATCH + TABLES, WORK, 0,
    )(partners, place, groups, middle, rim1, rim2, *inside, base)
    images, members = lax.axis_size("image"), lax.axis_size("swarm")
    shares = string_shares(image) / (members * GSIZE)
    part, shares = lax.optimization_barrier((part, shares))
    final_positions = final.reshape(1, 1, 3, 1, LANES * LANES)

    domains = lax.axis_size("domain")
    copies = call(
        spread_kernel, "spread", shape(members * domains, 1, 3 * LANES), [VMEM], [], 0, 100_000
    )(part)
    everyone = lax.all_to_all(copies, ("swarm", "domain"), split_axis=0, concat_axis=0, tiled=True)
    updated = jnp.sum(everyone, axis=0)
    up = [(i, (i + 1) % images) for i in range(images)]
    earlier = lax.ppermute(updated, "image", up)
    later = lax.ppermute(updated, "image", [(target, source) for source, target in up])
    new_string = shares[0] * updated + shares[1] * earlier + shares[2] * later
    new_string = new_string.reshape(1, 3, LANES)
    return (final_positions, new_string)


def solution(mesh):
    in_specs = (
        P("image", None, "domain", "swarm"),
        P("image", None, "domain", None, "swarm"),
        P("domain", None, None),
        P(),
    )
    out_specs = (P("image", "swarm", None, "domain", None), P("image", None, None))
    return jax.shard_map(
        on_device, mesh=mesh, in_specs=in_specs, out_specs=out_specs, check_vma=False
    )
```

```python
import functools

import jax
import jax.numpy as jnp
from jax import lax
from jax.experimental import pallas as pl
from jax.experimental.pallas import tpu as pltpu
from jax.sharding import PartitionSpec as P

HALO = 4096
GSIZE = 16
LANES = 128
ROWS = 8
LAG = 5
SLOTS = 16

time_step = 0.25
strength = 0.1
smoothing = 0.25

F32 = jnp.float32
BF16 = jnp.bfloat16


def three_parts(value):
    high = value.astype(BF16).astype(F32)
    rest = value - high
    middle = rest.astype(BF16).astype(F32)
    return high, middle, rest - middle


def two_parts(value):
    high = value.astype(BF16)
    return high, (value - high.astype(F32)).astype(BF16)


def put_rows(ref, rows):
    for place, row in enumerate(rows):
        ref[place * ROWS:(place + 1) * ROWS, :] = row


def build_group(field, rows_q, rows_v, columns, values, first):
    one, zero = jnp.ones((ROWS, LANES), F32), jnp.zeros((ROWS, LANES), F32)
    parts = [three_parts(x) for x in field]
    norm = three_parts(0.5 - 0.5 * (field[0] * field[0] + field[1] * field[1] + field[2] * field[2]))
    of_q = []
    for h, m, l in parts:
        of_q += [h, m, h, m, l, h]
    put_rows(rows_q, of_q + [one] * 3 + list(norm) + [zero] * 8)
    put_rows(
        rows_v,
        [p[0] for p in parts] + [one] + [p[2] for p in parts] + [zero]
        + [p[1] for p in parts] + [zero] * 5,
    )
    for t in range(ROWS):
        columns[first + t] = rows_q[pl.ds(t, 32, stride=ROWS), :].astype(BF16)
        values[first + t] = rows_v[pl.ds(t, 16, stride=ROWS), :].astype(BF16)


def put_own_rows(field, rows_p, first):
    one, zero = jnp.ones((ROWS, LANES), F32), jnp.zeros((ROWS, LANES), F32)
    norm = three_parts(0.5 - 0.5 * (field[0] * field[0] + field[1] * field[1] + field[2] * field[2]))
    of_p = []
    for x in field:
        h, m, l = three_parts(x)
        of_p += [h, h, m, m, h, l]
    put_rows(rows_p.at[pl.ds(first, 32 * ROWS)], of_p + list(norm) + [one] * 3 + [zero] * 8)


def forces(groups, field_ref, shift, pairs, rows_p, sums, weights, columns, values, emit):
    def place_of(n):
        group, t = divmod(n, ROWS)
        tile = groups[group] * ROWS + t
        others = [tile + HALO // LANES, pairs[0, tile], pairs[1, tile]]
        return group, t, [e - shift for e in others]

    def make_weights(n):
        group, t, others = place_of(n)
        if t == 0:
            put_own_rows([field_ref[groups[group], c] for c in range(3)], rows_p, group * 32 * ROWS)
        p_side = rows_p[pl.ds(group * 32 * ROWS + t, 32, stride=ROWS), :].astype(BF16)
        q_side = jnp.concatenate([columns[e] for e in others], axis=1)
        overlap = jnp.maximum(
            lax.dot_general(
                q_side, p_side, (((0,), (0,)), ((), ())), preferred_element_type=F32
            ),
            0.0,
        )
        high, low = two_parts(overlap * overlap)
        weights[n % SLOTS, :3 * LANES] = high
        weights[n % SLOTS, 3 * LANES:] = low

    def use_weights(n):
        group, t, others = place_of(n)
        q_values = jnp.concatenate([values[e] for e in others], axis=1)
        base = group * 16 * ROWS
        sums[base + t * 16:base + (t + 1) * 16, :] = jnp.dot(
            jnp.concatenate([q_values] * 2, axis=1), weights[n % SLOTS], preferred_element_type=F32
        )
        if t == ROWS - 1:
            row = lambda r: sums[pl.ds(base + r, ROWS, stride=16), :]
            total = row(3)
            for c in range(3):
                pulled = row(c) + row(8 + c) + row(4 + c)
                emit(groups[group], c, strength * (field_ref[groups[group], c] * total - pulled))

    count = len(groups) * ROWS
    for n in range(count + LAG):
        if n < count:
            make_weights(n)
        if n >= LAG:
            use_weights(n - LAG)


def inner_kernel(pairs, field_ref, out_ref, columns, values, rows_q, rows_v, rows_p, sums, weights):
    @pl.loop(0, 16)
    def _(s):
        build_group([field_ref[s, c] for c in range(3)], rows_q, rows_v, columns, values, s * ROWS)

    def emit(s, c, force):
        out_ref[s - 4, c] = force

    forces(
        range(4, 12), field_ref, HALO // LANES, pairs, rows_p, sums, weights, columns, values, emit
    )


def rim_forces(
    pairs, place, field_ref, rim_refs, own_tables, rows_q, rows_v, rows_p, sums, weights, columns, values, emit
):
    @pl.loop(0, 16)
    def _(s):
        for whole, own in ((columns, own_tables[0]), (values, own_tables[1])):
            whole[pl.ds(HALO // LANES + s * ROWS, ROWS)] = own[pl.ds(s * ROWS, ROWS)]

    odd, second = place[1], place[2] > 0
    for ref, first, exists in ((rim_refs[0], 20 * (1 - odd), None), (rim_refs[1], 20 * odd, second)):

        @pl.loop(0, 4)
        def _(s):
            field = [ref[s, c] for c in range(3)]
            if exists is not None:
                field = [jnp.where(exists, x, 0.0) for x in field]
            build_group(field, rows_q, rows_v, columns, values, (first + s) * ROWS)

    forces(
        (0, 1, 2, 3, 12, 13, 14, 15), field_ref, 0, pairs, rows_p, sums, weights, columns, values, emit
    )


def first_rim_kernel(
    pairs, place, field_ref, rim1_ref, rim2_ref, inner_ref, columns_ref, values_ref, vel_ref,
    middle_ref, base_ref, send1_ref, send2_ref,
    rows_q, rows_v, rows_p, sums, weights, columns, values,
):
    def step(s, c, force):
        velocity = vel_ref[s, c] + time_step * force
        middle = field_ref[s, c] + time_step * velocity
        middle_ref[s, c] = middle
        base_ref[s, c] = middle + time_step * velocity

    rim_forces(
        pairs, place, field_ref, (rim1_ref, rim2_ref), (columns_ref, values_ref),
        rows_q, rows_v, rows_p, sums, weights, columns, values, step,
    )
    for s in range(8):
        for c in range(3):
            step(s + 4, c, inner_ref[s, c])

    odd = place[1]
    send1_ref[...] = middle_ref[pl.ds(12 * (1 - odd), 4)]
    send2_ref[...] = middle_ref[pl.ds(12 * odd, 4)]


def second_rim_kernel(
    pairs, place, groups_ref, field_ref, rim1_ref, rim2_ref, inner_ref, columns_ref, values_ref,
    base_ref, final_ref, part_ref,
    rows_q, rows_v, rows_p, sums, weights, columns, values,
):
    def step(s, c, force):
        final_ref[c, pl.ds(s * ROWS, ROWS), :] = (
            base_ref[s, c] + (time_step * time_step) * force
        )

    rim_forces(
        pairs, place, field_ref, (rim1_ref, rim2_ref), (columns_ref, values_ref),
        rows_q, rows_v, rows_p, sums, weights, columns, values, step,
    )
    for s in range(8):
        for c in range(3):
            step(s + 4, c, inner_ref[s, c])

    local = groups_ref[...] - place[0] * (LANES * LANES)
    tile_of, lane_of = local >> 7, local & 127
    moving = jnp.concatenate(
        [jnp.concatenate(two_parts(final_ref[c].T), axis=1) for c in range(3)], axis=0
    )
    down = lax.broadcasted_iota(jnp.int32, (LANES, LANES), 0)
    total = jnp.zeros((3, ROWS, 2 * LANES), F32)
    for g in range(0, GSIZE, 2):
        pair = lambda rows: jnp.concatenate([down == rows[g + i:g + i + 1, :] for i in (0, 1)], axis=1)
        chosen = pair(tile_of).astype(F32).astype(BF16)
        here = pair(lane_of)
        found = jnp.dot(
            moving, jnp.concatenate([chosen] * 2, axis=0), preferred_element_type=F32
        )
        kept = jnp.where(jnp.concatenate([here] * 3, axis=0), found, 0.0)
        total = total + jnp.sum(kept.reshape(3, LANES // ROWS, ROWS, 2 * LANES), axis=1)
    for c in range(3):
        both = total[c, :, :LANES] + total[c, :, LANES:]
        part_ref[:, c * LANES:(c + 1) * LANES] = jnp.sum(both, axis=0, keepdims=True)


def fetch_kernel(pairs_ref, groups_ref, pairs_out, groups_out):
    pairs_out[...] = pairs_ref[...]
    groups_out[...] = groups_ref[...]


def spread_kernel(own_ref, out_ref):
    out_ref[...] = jnp.broadcast_to(own_ref[...][None], out_ref.shape)


def string_kernel(shares, own_ref, before_ref, after_ref, out_ref):
    mixed = shares[0] * own_ref[...] + shares[1] * before_ref[...] + shares[2] * after_ref[...]
    for c in range(3):
        out_ref[c] = mixed[:, c * LANES:(c + 1) * LANES]


def pack_kernel(vel_hbm, conf_hbm, out_ref, vel_ref, conf_ref, arrived):
    vel_copy = pltpu.make_async_copy(vel_hbm, vel_ref, arrived.at[0])
    conf_copy = pltpu.make_async_copy(conf_hbm, conf_ref, arrived.at[1])
    vel_copy.start()
    conf_copy.start()
    conf_copy.wait()
    for c in range(3):
        for m in range(16):
            out_ref[m * 48 + 24 + c * ROWS:m * 48 + 32 + c * ROWS, :] = conf_ref[c]
    vel_copy.wait()
    for c in range(3):
        for j in range(ROWS):
            for half in range(2):
                out_ref[pl.ds(half * 8 * 48 + c * ROWS + j, ROWS, stride=48), :] = vel_ref[
                    c, half * 8:half * 8 + 8, j * LANES:(j + 1) * LANES
                ]


VMEM = pl.BlockSpec(memory_space=pltpu.VMEM)
SMEM = pl.BlockSpec(memory_space=pltpu.SMEM)
ANY = pl.BlockSpec(memory_space=pl.ANY)


ROW_SCRATCH = [
    pltpu.VMEM((32 * ROWS, LANES), F32),
    pltpu.VMEM((16 * ROWS, LANES), F32),
    pltpu.VMEM((8 * 32 * ROWS, LANES), F32),
    pltpu.VMEM((8 * 16 * ROWS, LANES), F32),
    pltpu.VMEM((SLOTS, 6 * LANES, LANES), BF16),
]
TABLES = [pltpu.VMEM((192, 32, LANES), BF16), pltpu.VMEM((192, 16, LANES), BF16)]


def call(kernel, name, out, specs, scratches, flops, moved, vmem=40 * 1024 * 1024):
    return pl.pallas_call(
        kernel,
        out_shape=out,
        in_specs=specs,
        out_specs=jax.tree.map(lambda _: VMEM, out),
        scratch_shapes=scratches,
        compiler_params=pltpu.CompilerParams(vmem_limit_bytes=vmem),
        cost_estimate=pl.CostEstimate(flops=flops, bytes_accessed=moved, transcendentals=0),
        name=name,
    )


WORK = 8_000_000_000


def shape(*dims):
    return jax.ShapeDtypeStruct(dims, F32)


def swap_rims(first, second):
    count = lax.axis_size("domain")
    inside = [(i, i ^ 1) for i in range(count)]
    across = [(i, (i + 1 if i % 2 else i - 1) % count) for i in range(count)]
    return lax.ppermute(first, "domain", inside), lax.ppermute(second, "domain", across)


def string_shares(place):
    before = (place > 0).astype(F32) * smoothing
    after = (place < lax.axis_size("image") - 1).astype(F32) * smoothing
    return jnp.stack([1.0 - before - after, before, after])


def on_device(configuration, velocities, pairs, cv_atoms):
    partners = pairs[0].T
    groups = cv_atoms.T
    configuration, velocities, domain, image = lax.optimization_barrier(
        (configuration, velocities, lax.axis_index("domain"), lax.axis_index("image"))
    )
    packed = call(
        pack_kernel, "pack", shape(16 * 48, LANES), [ANY, ANY],
        [
            pltpu.VMEM((3, 16, 1024), F32),
            pltpu.VMEM((3, ROWS, LANES), F32),
            pltpu.SemaphoreType.DMA((2,)),
        ],
        0, 600_000, 62_900_000,
    )(velocities.reshape(3, 16, 1024), configuration.reshape(3, ROWS, LANES))
    got = lax.all_to_all(
        packed.reshape(16, 6, ROWS, LANES), "swarm", split_axis=0, concat_axis=0, tiled=True
    )
    partners, groups = call(
        fetch_kernel, "fetch",
        (jax.ShapeDtypeStruct((2, LANES), jnp.int32), jax.ShapeDtypeStruct((GSIZE, LANES), jnp.int32)),
        [VMEM, VMEM], [], 0, 20_000,
    )(partners, groups)
    got, domain, image, partners, groups = lax.optimization_barrier(
        (got, domain, image, partners, groups)
    )
    start_vel, start_pos = got[:, :3], got[:, 3:]
    odd = domain % 2
    inner_domain = (domain > 0) & (domain < lax.axis_size("domain") - 1)
    place = jnp.stack([domain, odd, inner_domain.astype(domain.dtype)])

    whole, rim = shape(16, 3, ROWS, LANES), shape(4, 3, ROWS, LANES)
    tables = (
        jax.ShapeDtypeStruct((128, 32, LANES), BF16), jax.ShapeDtypeStruct((128, 16, LANES), BF16)
    )
    inner = call(
        inner_kernel, "inner", (shape(8, 3, ROWS, LANES),) + tables, [SMEM, VMEM], ROW_SCRATCH, WORK, 0
    )
    rim1, rim2 = swap_rims(
        lax.dynamic_slice_in_dim(start_pos, 12 * (1 - odd), 4, 0),
        lax.dynamic_slice_in_dim(start_pos, 12 * odd, 4, 0),
    )
    inside = inner(partners, start_pos)
    middle, base, send1, send2 = call(
        first_rim_kernel, "first_rim", (whole, whole, rim, rim), [SMEM, SMEM] + [VMEM] * 7,
        ROW_SCRATCH + TABLES, WORK, 0,
    )(partners, place, start_pos, rim1, rim2, *inside, start_vel)

    rim1, rim2 = swap_rims(send1, send2)
    inside = inner(partners, middle)
    final, part = call(
        second_rim_kernel, "second_rim", (shape(3, LANES, LANES), shape(1, 3 * LANES)),
        [SMEM, SMEM] + [VMEM] * 8, ROW_SCRATCH + TABLES, WORK, 0,
    )(partners, place, groups, middle, rim1, rim2, *inside, base)
    images, members = lax.axis_size("image"), lax.axis_size("swarm")
    shares = string_shares(image) / (members * GSIZE)
    part, shares = lax.optimization_barrier((part, shares))
    final_positions = final.reshape(1, 1, 3, 1, LANES * LANES)

    domains = lax.axis_size("domain")
    copies = call(
        spread_kernel, "spread", shape(members * domains, 1, 3 * LANES), [VMEM], [], 0, 100_000
    )(part)
    everyone = lax.all_to_all(copies, ("swarm", "domain"), split_axis=0, concat_axis=0, tiled=True)
    updated = jnp.sum(everyone, axis=0)
    up = [(i, (i + 1) % images) for i in range(images)]
    earlier = lax.ppermute(updated, "image", up)
    later = lax.ppermute(updated, "image", [(target, source) for source, target in up])
    new_string = call(
        string_kernel, "string", shape(3, 1, LANES), [SMEM] + [VMEM] * 3, [], 0, 10_000
    )(shares, updated, earlier, later)
    new_string = new_string.transpose(1, 0, 2)
    return (final_positions, new_string)


def solution(mesh):
    in_specs = (
        P("image", None, "domain", "swarm"),
        P("image", None, "domain", None, "swarm"),
        P("domain", None, None),
        P(),
    )
    out_specs = (P("image", "swarm", None, "domain", None), P("image", None, None))
    return jax.shard_map(
        on_device, mesh=mesh, in_specs=in_specs, out_specs=out_specs, check_vma=False
    )
```

```python
import functools

import jax
import jax.numpy as jnp
from jax import lax
from jax.experimental import pallas as pl
from jax.experimental.pallas import tpu as pltpu
from jax.sharding import PartitionSpec as P

HALO = 4096
GSIZE = 16
LANES = 128
ROWS = 8
LAG = 5
SLOTS = 16

time_step = 0.25
strength = 0.1
smoothing = 0.25

F32 = jnp.float32
BF16 = jnp.bfloat16


def three_parts(value):
    high = value.astype(BF16).astype(F32)
    rest = value - high
    middle = rest.astype(BF16).astype(F32)
    return high, middle, rest - middle


def two_parts(value):
    high = value.astype(BF16)
    return high, (value - high.astype(F32)).astype(BF16)


def put_rows(ref, rows):
    for place, row in enumerate(rows):
        ref[place * ROWS:(place + 1) * ROWS, :] = row


def build_group(field, rows_q, rows_v, columns, values, first):
    one, zero = jnp.ones((ROWS, LANES), F32), jnp.zeros((ROWS, LANES), F32)
    parts = [three_parts(x) for x in field]
    norm = three_parts(0.5 - 0.5 * (field[0] * field[0] + field[1] * field[1] + field[2] * field[2]))
    of_q = []
    for h, m, l in parts:
        of_q += [h, m, h, m, l, h]
    put_rows(rows_q, of_q + [one] * 3 + list(norm) + [zero] * 8)
    put_rows(
        rows_v,
        [p[0] for p in parts] + [one] + [p[2] for p in parts] + [zero]
        + [p[1] for p in parts] + [zero] * 5,
    )
    for t in range(ROWS):
        columns[first + t] = rows_q[pl.ds(t, 32, stride=ROWS), :].astype(BF16)
        values[first + t] = rows_v[pl.ds(t, 16, stride=ROWS), :].astype(BF16)


def put_own_rows(field, rows_p, first):
    one, zero = jnp.ones((ROWS, LANES), F32), jnp.zeros((ROWS, LANES), F32)
    norm = three_parts(0.5 - 0.5 * (field[0] * field[0] + field[1] * field[1] + field[2] * field[2]))
    of_p = []
    for x in field:
        h, m, l = three_parts(x)
        of_p += [h, h, m, m, h, l]
    put_rows(rows_p.at[pl.ds(first, 32 * ROWS)], of_p + list(norm) + [one] * 3 + [zero] * 8)


def forces(groups, field_ref, shift, pairs, rows_p, sums, weights, columns, values, emit):
    def place_of(n):
        group, t = divmod(n, ROWS)
        tile = groups[group] * ROWS + t
        others = [tile + HALO // LANES, pairs[0, tile], pairs[1, tile]]
        return group, t, [e - shift for e in others]

    def make_weights(n):
        group, t, others = place_of(n)
        if t == 0:
            put_own_rows([field_ref[groups[group], c] for c in range(3)], rows_p, group * 32 * ROWS)
        p_side = rows_p[pl.ds(group * 32 * ROWS + t, 32, stride=ROWS), :].astype(BF16)
        q_side = jnp.concatenate([columns[e] for e in others], axis=1)
        overlap = jnp.maximum(
            lax.dot_general(
                q_side, p_side, (((0,), (0,)), ((), ())), preferred_element_type=F32
            ),
            0.0,
        )
        high, low = two_parts(overlap * overlap)
        weights[n % SLOTS, :3 * LANES] = high
        weights[n % SLOTS, 3 * LANES:] = low

    def use_weights(n):
        group, t, others = place_of(n)
        q_values = jnp.concatenate([values[e] for e in others], axis=1)
        base = group * 16 * ROWS
        sums[base + t * 16:base + (t + 1) * 16, :] = jnp.dot(
            jnp.concatenate([q_values] * 2, axis=1), weights[n % SLOTS], preferred_element_type=F32
        )
        if t == ROWS - 1:
            row = lambda r: sums[pl.ds(base + r, ROWS, stride=16), :]
            total = row(3)
            for c in range(3):
                pulled = row(c) + row(8 + c) + row(4 + c)
                emit(groups[group], c, strength * (field_ref[groups[group], c] * total - pulled))

    count = len(groups) * ROWS
    for n in range(count + LAG):
        if n < count:
            make_weights(n)
        if n >= LAG:
            use_weights(n - LAG)


def inner_kernel(pairs, field_ref, out_ref, columns, values, rows_q, rows_v, rows_p, sums, weights):
    @pl.loop(0, 16)
    def _(s):
        build_group([field_ref[s, c] for c in range(3)], rows_q, rows_v, columns, values, s * ROWS)

    def emit(s, c, force):
        out_ref[s - 4, c] = force

    forces(
        range(4, 12), field_ref, HALO // LANES, pairs, rows_p, sums, weights, columns, values, emit
    )


def rim_forces(
    pairs, place, field_ref, rim_refs, own_tables, rows_q, rows_v, rows_p, sums, weights, columns, values, emit
):
    @pl.loop(0, 16)
    def _(s):
        for whole, own in ((columns, own_tables[0]), (values, own_tables[1])):
            whole[pl.ds(HALO // LANES + s * ROWS, ROWS)] = own[pl.ds(s * ROWS, ROWS)]

    odd, second = place[1], place[2] > 0
    for ref, first, exists in ((rim_refs[0], 20 * (1 - odd), None), (rim_refs[1], 20 * odd, second)):

        @pl.loop(0, 4)
        def _(s):
            field = [ref[s, c] for c in range(3)]
            if exists is not None:
                field = [jnp.where(exists, x, 0.0) for x in field]
            build_group(field, rows_q, rows_v, columns, values, (first + s) * ROWS)

    forces(
        (0, 1, 2, 3, 12, 13, 14, 15), field_ref, 0, pairs, rows_p, sums, weights, columns, values, emit
    )


def first_rim_kernel(
    pairs, place, field_ref, rim1_ref, rim2_ref, inner_ref, columns_ref, values_ref, vel_ref,
    middle_ref, base_ref, send1_ref, send2_ref,
    rows_q, rows_v, rows_p, sums, weights, columns, values,
):
    def step(s, c, force):
        velocity = vel_ref[s, c] + time_step * force
        middle = field_ref[s, c] + time_step * velocity
        middle_ref[s, c] = middle
        base_ref[s, c] = middle + time_step * velocity

    rim_forces(
        pairs, place, field_ref, (rim1_ref, rim2_ref), (columns_ref, values_ref),
        rows_q, rows_v, rows_p, sums, weights, columns, values, step,
    )
    for s in range(8):
        for c in range(3):
            step(s + 4, c, inner_ref[s, c])

    odd = place[1]
    send1_ref[...] = middle_ref[pl.ds(12 * (1 - odd), 4)]
    send2_ref[...] = middle_ref[pl.ds(12 * odd, 4)]


def second_rim_kernel(
    pairs, place, groups_ref, field_ref, rim1_ref, rim2_ref, inner_ref, columns_ref, values_ref,
    base_ref, final_ref, part_ref,
    rows_q, rows_v, rows_p, sums, weights, columns, values,
):
    def step(s, c, force):
        final_ref[c, pl.ds(s * ROWS, ROWS), :] = (
            base_ref[s, c] + (time_step * time_step) * force
        )

    rim_forces(
        pairs, place, field_ref, (rim1_ref, rim2_ref), (columns_ref, values_ref),
        rows_q, rows_v, rows_p, sums, weights, columns, values, step,
    )
    for s in range(8):
        for c in range(3):
            step(s + 4, c, inner_ref[s, c])

    local = groups_ref[...] - place[0] * (LANES * LANES)
    tile_of, lane_of = local >> 7, local & 127
    moving = jnp.concatenate(
        [jnp.concatenate(two_parts(final_ref[c].T), axis=1) for c in range(3)], axis=0
    )
    down = lax.broadcasted_iota(jnp.int32, (LANES, LANES), 0)
    total = jnp.zeros((3, ROWS, 2 * LANES), F32)
    for g in range(0, GSIZE, 2):
        pair = lambda rows: jnp.concatenate([down == rows[g + i:g + i + 1, :] for i in (0, 1)], axis=1)
        chosen = pair(tile_of).astype(F32).astype(BF16)
        here = pair(lane_of)
        found = jnp.dot(
            moving, jnp.concatenate([chosen] * 2, axis=0), preferred_element_type=F32
        )
        kept = jnp.where(jnp.concatenate([here] * 3, axis=0), found, 0.0)
        total = total + jnp.sum(kept.reshape(3, LANES // ROWS, ROWS, 2 * LANES), axis=1)
    for c in range(3):
        both = total[c, :, :LANES] + total[c, :, LANES:]
        part_ref[:, c * LANES:(c + 1) * LANES] = jnp.sum(both, axis=0, keepdims=True)


def fetch_kernel(pairs_ref, groups_ref, pairs_out, groups_out):
    pairs_out[...] = pairs_ref[...]
    groups_out[...] = groups_ref[...]


def spread_kernel(own_ref, out_ref):
    out_ref[...] = jnp.broadcast_to(own_ref[...][None], out_ref.shape)


def pack_kernel(vel_hbm, conf_hbm, out_ref, vel_ref, conf_ref, arrived):
    vel_copy = pltpu.make_async_copy(vel_hbm, vel_ref, arrived.at[0])
    conf_copy = pltpu.make_async_copy(conf_hbm, conf_ref, arrived.at[1])
    vel_copy.start()
    conf_copy.start()
    conf_copy.wait()
    for c in range(3):
        for m in range(16):
            out_ref[m * 48 + 24 + c * ROWS:m * 48 + 32 + c * ROWS, :] = conf_ref[c]
    vel_copy.wait()
    for c in range(3):
        for j in range(ROWS):
            for half in range(2):
                out_ref[pl.ds(half * 8 * 48 + c * ROWS + j, ROWS, stride=48), :] = vel_ref[
                    c, half * 8:half * 8 + 8, j * LANES:(j + 1) * LANES
                ]


VMEM = pl.BlockSpec(memory_space=pltpu.VMEM)
SMEM = pl.BlockSpec(memory_space=pltpu.SMEM)
ANY = pl.BlockSpec(memory_space=pl.ANY)


ROW_SCRATCH = [
    pltpu.VMEM((32 * ROWS, LANES), F32),
    pltpu.VMEM((16 * ROWS, LANES), F32),
    pltpu.VMEM((8 * 32 * ROWS, LANES), F32),
    pltpu.VMEM((8 * 16 * ROWS, LANES), F32),
    pltpu.VMEM((SLOTS, 6 * LANES, LANES), BF16),
]
TABLES = [pltpu.VMEM((192, 32, LANES), BF16), pltpu.VMEM((192, 16, LANES), BF16)]


def call(kernel, name, out, specs, scratches, flops, moved, vmem=40 * 1024 * 1024):
    return pl.pallas_call(
        kernel,
        out_shape=out,
        in_specs=specs,
        out_specs=jax.tree.map(lambda _: VMEM, out),
        scratch_shapes=scratches,
        compiler_params=pltpu.CompilerParams(vmem_limit_bytes=vmem),
        cost_estimate=pl.CostEstimate(flops=flops, bytes_accessed=moved, transcendentals=0),
        name=name,
    )


WORK = 8_000_000_000


def shape(*dims):
    return jax.ShapeDtypeStruct(dims, F32)


def swap_rims(first, second):
    count = lax.axis_size("domain")
    inside = [(i, i ^ 1) for i in range(count)]
    across = [(i, (i + 1 if i % 2 else i - 1) % count) for i in range(count)]
    return lax.ppermute(first, "domain", inside), lax.ppermute(second, "domain", across)


def string_shares(place):
    before = (place > 0).astype(F32) * smoothing
    after = (place < lax.axis_size("image") - 1).astype(F32) * smoothing
    return 1.0 - before - after, before, after


def on_device(configuration, velocities, pairs, cv_atoms):
    partners = pairs[0].T
    groups = cv_atoms.T
    configuration, velocities, domain, image = lax.optimization_barrier(
        (configuration, velocities, lax.axis_index("domain"), lax.axis_index("image"))
    )
    packed = call(
        pack_kernel, "pack", shape(16 * 48, LANES), [ANY, ANY],
        [
            pltpu.VMEM((3, 16, 1024), F32),
            pltpu.VMEM((3, ROWS, LANES), F32),
            pltpu.SemaphoreType.DMA((2,)),
        ],
        0, 600_000, 62_900_000,
    )(velocities.reshape(3, 16, 1024), configuration.reshape(3, ROWS, LANES))
    got = lax.all_to_all(
        packed.reshape(16, 6, ROWS, LANES), "swarm", split_axis=0, concat_axis=0, tiled=True
    )
    partners, groups = call(
        fetch_kernel, "fetch",
        (jax.ShapeDtypeStruct((2, LANES), jnp.int32), jax.ShapeDtypeStruct((GSIZE, LANES), jnp.int32)),
        [VMEM, VMEM], [], 0, 20_000,
    )(partners, groups)
    got, domain, image, partners, groups = lax.optimization_barrier(
        (got, domain, image, partners, groups)
    )
    start_vel, start_pos = got[:, :3], got[:, 3:]
    odd = domain % 2
    inner_domain = (domain > 0) & (domain < lax.axis_size("domain") - 1)
    place = jnp.stack([domain, odd, inner_domain.astype(domain.dtype)])

    whole, rim = shape(16, 3, ROWS, LANES), shape(4, 3, ROWS, LANES)
    tables = (
        jax.ShapeDtypeStruct((128, 32, LANES), BF16), jax.ShapeDtypeStruct((128, 16, LANES), BF16)
    )
    inner = call(
        inner_kernel, "inner", (shape(8, 3, ROWS, LANES),) + tables, [SMEM, VMEM], ROW_SCRATCH, WORK, 0
    )
    rim1, rim2 = swap_rims(
        lax.dynamic_slice_in_dim(start_pos, 12 * (1 - odd), 4, 0),
        lax.dynamic_slice_in_dim(start_pos, 12 * odd, 4, 0),
    )
    inside = inner(partners, start_pos)
    middle, base, send1, send2 = call(
        first_rim_kernel, "first_rim", (whole, whole, rim, rim), [SMEM, SMEM] + [VMEM] * 7,
        ROW_SCRATCH + TABLES, WORK, 0,
    )(partners, place, start_pos, rim1, rim2, *inside, start_vel)

    rim1, rim2 = swap_rims(send1, send2)
    inside = inner(partners, middle)
    final, part = call(
        second_rim_kernel, "second_rim", (shape(3, LANES, LANES), shape(1, 3 * LANES)),
        [SMEM, SMEM] + [VMEM] * 8, ROW_SCRATCH + TABLES, WORK, 0,
    )(partners, place, groups, middle, rim1, rim2, *inside, base)
    images, members = lax.axis_size("image"), lax.axis_size("swarm")
    shares = tuple(share / (members * GSIZE) for share in string_shares(image))
    part, shares = lax.optimization_barrier((part, shares))
    final_positions = final.reshape(1, 1, 3, 1, LANES * LANES)

    domains = lax.axis_size("domain")
    copies = call(
        spread_kernel, "spread", shape(members * domains, 1, 3 * LANES), [VMEM], [], 0, 100_000
    )(part)
    everyone = lax.all_to_all(copies, ("swarm", "domain"), split_axis=0, concat_axis=0, tiled=True)
    updated = jnp.sum(everyone, axis=0)
    up = [(i, (i + 1) % images) for i in range(images)]
    earlier = lax.ppermute(updated, "image", up)
    later = lax.ppermute(updated, "image", [(target, source) for source, target in up])
    new_string = shares[0] * updated + shares[1] * earlier + shares[2] * later
    new_string = new_string.reshape(1, 3, LANES)
    return (final_positions, new_string)


def solution(mesh):
    in_specs = (
        P("image", None, "domain", "swarm"),
        P("image", None, "domain", None, "swarm"),
        P("domain", None, None),
        P(),
    )
    out_specs = (P("image", "swarm", None, "domain", None), P("image", None, None))
    return jax.shard_map(
        on_device, mesh=mesh, in_specs=in_specs, out_specs=out_specs, check_vma=False
    )
```
